256 devices in a mesh: bg: 64 (over z, x, core), type: 4 (over y).
Axes of the slice: x: 4, y: 4, z: 8, core: 2. Of those that a mesh axis runs over, the one named last changes fastest.
Arguments:
- seed_slab: float32 [8192, 36864], P('bg', 'type'), as said below
- row_target: int32 [8192], P('bg'), may hold values from 50 to 1999
- county_id: int32 [8192], P('bg'), may hold values from 0 to 63, as said below
- county_target: int32 [64, 36864], P(None, 'type'), may hold values from 1 to 999
Outputs:
- fitted: float32 [8192, 36864], P('bg', 'type')
The draws below stay inside these ranges and needn't reach their ends.
Inputs may be any that keep to these rules, and one draw needn't show every extreme that they name: county_id never falls along the block groups, and every county 0 to 63 has one or more block groups. `seed_slab`: positive.
All inputs are finite; a program needn't handle non-finite values.
Results may differ from the reference program's by a relative error of at most 0.0001.
Values sent between devices are 32-bit elements; how exact they have to be, the bound alone decides.
No kernel may reach another device: no remote copies, remote signals or barrier semaphores. Data moves between devices by JAX's collectives and lax.ppermute only.
A program may use at most 64 MiB of HBM per device.

```python
import jax
import jax.numpy as jnp

TYPES = 36864
COUNTIES = 64
CYCLES = 2
GROUPS = 8192


def draw_seed_slab(key, part):
    key = jax.random.fold_in(key, 11)
    row_key, col_key, noise_key = jax.random.split(key, 3)
    row_scale = jnp.exp(jax.random.uniform(row_key, (GROUPS, 1), jnp.float32) * jnp.log(10.0))
    col_scale = jnp.exp(jax.random.uniform(col_key, (1, TYPES), jnp.float32) * jnp.log(10.0))
    noise = jnp.exp(jax.random.uniform(noise_key, (GROUPS, TYPES), jnp.float32, -4.0, 4.0))
    return (row_scale * col_scale * noise).astype(jnp.float32)


def draw_county_id(key, part):
    key = jax.random.fold_in(key, 23)
    first_cut = GROUPS // 4
    cuts = jax.random.permutation(key, GROUPS - first_cut)[:COUNTIES - 1] + first_cut
    positions = jnp.arange(GROUPS, dtype=jnp.int32)
    return jnp.sum((positions[:, None] >= cuts[None, :]).astype(jnp.int32), axis=1).astype(jnp.int32)


def with_ends(result, stream_key, least, high):
    extent = result.shape
    index_at = [jax.random.randint(jax.random.fold_in(stream_key, axis), (), 0, extent[axis]) for axis in range(len(extent))]
    result = result.at[tuple(index_at)].set(least)
    longest = extent.index(max(extent))
    index_at[longest] = (index_at[longest] + 1) % extent[longest]
    return result.at[tuple(index_at)].set(high)


def setup_inputs(seed: int = 0) -> dict:
    arg_keys = jax.random.split(jax.random.key(seed), 5)
    seed_slab = draw_seed_slab(jax.random.fold_in(arg_keys[4], 71), 0)
    row_target = with_ends(jax.random.randint(arg_keys[1], (GROUPS,), 50, 2000), jax.random.fold_in(arg_keys[1], 1), 50, 1999).astype(jnp.int32)
    county_id = draw_county_id(jax.random.fold_in(arg_keys[4], 71), 0)
    county_target = with_ends(jax.random.randint(arg_keys[3], (COUNTIES, TYPES), 1, 1000), jax.random.fold_in(arg_keys[3], 1), 1, 999).astype(jnp.int32)
    return dict(seed_slab=seed_slab, row_target=row_target, county_id=county_id, county_target=county_target)


def reference(seed_slab, row_target, county_id, county_target):
    row_goal = row_target.astype(jnp.float32)
    people = jax.ops.segment_sum(row_goal, county_id, num_segments=COUNTIES)
    shares = county_target.astype(jnp.float32)
    share_total = jnp.sum(shares, axis=1)
    county_goal = shares * (people / share_total)[:, None]
    weights = seed_slab
    for cycle in range(CYCLES):
        row_sum = jnp.sum(weights, axis=1)
        weights = weights * (row_goal / row_sum)[:, None]
        county_sum = jax.ops.segment_sum(weights, county_id, num_segments=COUNTIES)
        weights = weights * (county_goal / county_sum)[county_id]
    return 100.0 * weights
```

```python
import functools

import jax
import jax.numpy as jnp
from jax import lax
from jax.experimental import pallas as pl
from jax.experimental.pallas import tpu as pltpu
from jax.sharding import PartitionSpec as P

LANES = 128
SUB = 8
PLANE = 8
CHUNKS = 4
COUNT = 255
NAMES = 128
VMEM_LIMIT = 40 * 1024 * 1024
VMEM = pl.BlockSpec(memory_space=pltpu.VMEM)
SMEM = pl.BlockSpec(memory_space=pltpu.SMEM)
PARAMS = pltpu.CompilerParams(vmem_limit_bytes=VMEM_LIMIT)


def f32(*shape):
    return jax.ShapeDtypeStruct(shape, jnp.float32)


def tile(t):
    return pl.ds(t * LANES, LANES)


def rows_of(b):
    return pl.ds(pl.multiple_of(b * SUB, SUB), SUB)


def column(row):
    return jnp.broadcast_to(row, (LANES, LANES)).T


def fold(parts):
    sub = lax.broadcasted_iota(jnp.int32, (SUB, LANES), 0)
    order, step = list(parts), 1
    while step < SUB:
        mask = (sub & step) == 0
        merged = []
        for a, b in zip(order[0::2], order[1::2]):
            merged.append(jnp.where(mask, a, b) + pltpu.roll(jnp.where(mask, b, a), SUB - step, 0))
        order, step = merged, 2 * step
    return order[0]


def seg_blocks(seg_ref, k):
    first = seg_ref[k]
    end = seg_ref[k + 1]
    return first >> 3, (end + 7) >> 3, seg_ref[NAMES + k]


def first_kernel(tiles, cid_ref, cid_row, goal_row, w_ref, tgt_ref, msg_ref, seg_ref, cols_ref, acc_w, acc_t):
    step = pl.program_id(0)

    @pl.when(step == 0)
    def _():
        rows = cid_ref.shape[0]

        def scan(g, n):
            c = cid_ref[g]
            new = jnp.logical_or(g == 0, c != cid_ref[jnp.maximum(g - 1, 0)])

            @pl.when(new)
            def _():
                seg_ref[n] = g
                seg_ref[NAMES + n] = c

            return n + new.astype(jnp.int32)

        n = lax.fori_loop(0, rows, scan, 0)
        seg_ref[n] = rows
        seg_ref[COUNT] = n
        cols_ref[0] = column(cid_row[...].astype(jnp.float32))
        cols_ref[1] = column(goal_row[...].astype(jnp.float32))
        acc_w[...] = jnp.zeros_like(acc_w)
        acc_t[...] = jnp.zeros_like(acc_t)

    for b in range(acc_w.shape[0] // SUB):
        rows = slice(b * SUB, (b + 1) * SUB)
        acc = acc_w[rows, :]
        for t in range(tiles):
            acc = acc + w_ref[rows, t * LANES : (t + 1) * LANES]
        acc_w[rows, :] = acc
    for b in range(tgt_ref.shape[0] // SUB):
        rows = slice(b * SUB, (b + 1) * SUB)
        acc = acc_t[rows, :]
        for t in range(tiles):
            acc = acc + tgt_ref[rows, t * LANES : (t + 1) * LANES].astype(jnp.float32)
        acc_t[rows, :] = acc

    @pl.when(step == pl.num_programs(0) - 1)
    def _():
        row_sum = jnp.sum(acc_w[...].T, axis=0, keepdims=True)
        share = jnp.sum(acc_t[...].T, axis=0, keepdims=True)
        message(msg_ref, row_sum, share)


def message(msg_ref, row_sum, share):
    sub = lax.broadcasted_iota(jnp.int32, (SUB, LANES), 0)
    block = jnp.where(sub == 0, row_sum, jnp.where(sub == 1, share, 0.0))
    for d in range(msg_ref.shape[0]):
        msg_ref[d] = block


def received(recv_ref):
    total = recv_ref[0]
    for d in range(1, recv_ref.shape[0]):
        total = total + recv_ref[d]
    return total


def sums_kernel(second, *refs):
    if second:
        seg_ref, recv_ref, goal_row, w_ref, cols_ref, r1_ref, fac_ref, send_ref, sums_ref, rcol_ref = refs
    else:
        seg_ref, recv_ref, goal_row, w_ref, cols_ref, send_ref, sums_ref, rcol_ref = refs
    tiles = w_ref.shape[1] // LANES
    half = tiles // 2
    width = tiles // CHUNKS
    rcol_ref[...] = column(goal_row[...].astype(jnp.float32) / received(recv_ref)[0:1])
    n = seg_ref[COUNT]
    sub = lax.broadcasted_iota(jnp.int32, (SUB, LANES), 0)

    def county(k, carry):
        b0, b1, c = seg_blocks(seg_ref, k)
        name = c.astype(jnp.float32)

        def persons(b, acc):
            rows = rows_of(b)
            return acc + jnp.where(cols_ref[0, rows, :] == name, cols_ref[1, rows, :], 0.0)

        people = jnp.sum(lax.fori_loop(b0, b1, persons, jnp.zeros((SUB, LANES), jnp.float32)), axis=0, keepdims=True)
        sums_ref[k, tiles : tiles + SUB, :] = jnp.where(sub == 0, people, jnp.where(sub == 1, name, 0.0))
        parts = []
        for q in range(CHUNKS):
            own = range(q * width, (q + 1) * width)
            if second:
                factor = [jnp.broadcast_to(fac_ref[k, t : t + 1, :], (SUB, LANES)) for t in own]

            def block(b, accs):
                rows = rows_of(b)
                mask = cols_ref[0, rows, :] == name
                out = []
                if second:
                    r1 = jnp.where(mask, r1_ref[rows, :], 0.0)
                    r2 = rcol_ref[rows, :]
                    for i, t in enumerate(own):
                        out.append(accs[i] + w_ref[rows, tile(t)] * r1 * factor[i] * r2)
                else:
                    r1 = jnp.where(mask, rcol_ref[rows, :], 0.0)
                    for i, t in enumerate(own):
                        out.append(accs[i] + w_ref[rows, tile(t)] * r1)
                return tuple(out)

            parts.extend(lax.fori_loop(b0, b1, block, tuple(jnp.zeros((SUB, LANES), jnp.float32) for _ in own)))
            while len(parts) >= SUB:
                at = (q + 1) * width - len(parts)
                sums_ref[k, at : at + SUB, :] = fold(parts[:SUB])
                parts = parts[SUB:]
        return carry

    lax.fori_loop(0, n, county, 0)
    for d in range(PLANE):
        h = d % 2
        for e, k in ((0, 0), (1, n - 1)):
            send_ref[d, e, 0:half, :] = sums_ref[k, h * half : (h + 1) * half, :]
            send_ref[d, e, half : half + 4, :] = sums_ref[k, tiles : tiles + 4, :]


def plane_kernel(got_ref, send_ref):
    planes, rows = send_ref.shape[:2]
    z = lax.axis_index("bg") // PLANE
    name = rows - 3
    first = got_ref[0, 0, name : name + 1, :]
    last = got_ref[PLANE - 1, 1, name : name + 1, :]
    head = jnp.zeros((rows, LANES), jnp.float32)
    tail = head
    for j in range(PLANE):
        head = head + jnp.where(got_ref[j, 0, name : name + 1, :] == first, got_ref[j, 0], 0.0)
        tail = tail + jnp.where(got_ref[j, 1, name : name + 1, :] == last, got_ref[j, 1], 0.0)
    sub = lax.broadcasted_iota(jnp.int32, (rows, LANES), 0)
    head = jnp.where(sub == name, first, head)
    tail = jnp.where(sub == name, last, tail)
    for j in range(planes):

        @pl.when(j > z)
        def _():
            send_ref[j] = tail

        @pl.when(j <= z)
        def _():
            send_ref[j] = head


def edge_kernel(got_ref, far_ref, own_ref, other_ref):
    planes, rows = far_ref.shape[:2]
    me = lax.axis_index("bg")
    z = me // PLANE
    here = me % PLANE
    name = rows - 3
    sub = lax.broadcasted_iota(jnp.int32, (rows, LANES), 0)

    for out_ref, i in ((own_ref, here), (other_ref, here ^ 1)):
        for e in range(2):
            mine = got_ref[i, e]
            county = got_ref[i, e, name : name + 1, :]
            total = mine
            for j in range(PLANE):
                side = jnp.where(j < i, 1, 0)
                hit = jnp.logical_and(got_ref[j, side, name : name + 1, :] == county, j != i)
                total = total + jnp.where(hit, got_ref[j, side], 0.0)
            for j in range(planes):
                hit = jnp.logical_and(far_ref[j, name : name + 1, :] == county, j != z)
                total = total + jnp.where(hit, far_ref[j], 0.0)
            out_ref[e] = jnp.where(sub == name, county, total)


def factors(seg_ref, recv_ref, sums_ref, own_ref, other_ref, tgt_ref, fac_ref, edge_ref, share_ref):
    tiles = tgt_ref.shape[1] // LANES
    half = tiles // 2
    core = lax.axis_index("bg") % 2
    n = seg_ref[COUNT]
    share = received(recv_ref)[1:2]
    lane = lax.broadcasted_iota(jnp.int32, (1, LANES), 1)
    sub = lax.broadcasted_iota(jnp.int32, (SUB, LANES), 0)

    for mine, left_ref, right_ref in ((0, own_ref, other_ref), (1, other_ref, own_ref)):

        @pl.when(core == mine)
        def _():
            for e in range(2):
                edge_ref[e, 0:half, :] = left_ref[e, 0:half, :]
                edge_ref[e, half:tiles, :] = right_ref[e, 0:half, :]
                edge_ref[e, tiles : tiles + 4, :] = left_ref[e, half : half + 4, :]

    def factor(k, total_ref):
        c = seg_ref[NAMES + k]
        rows = rows_of(c >> 3)
        mask = sub == (c & 7)
        for t in range(0, tiles, SUB):
            parts = [jnp.where(mask, tgt_ref[rows, tile(t + i)].astype(jnp.float32), 0.0) for i in range(SUB)]
            share_ref[t : t + SUB, :] = fold(parts)
        whole = jnp.sum(jnp.where(lane == c, share, 0.0), axis=1, keepdims=True)
        scale = total_ref[tiles : tiles + 1, :] / whole
        fac_ref[k] = share_ref[...] * scale / total_ref[0:tiles, :]

    factor(0, edge_ref.at[0])
    factor(n - 1, edge_ref.at[1])

    @pl.loop(1, n - 1)
    def _(k):
        factor(k, sums_ref.at[k])


def rows_kernel(
    seg_ref, recv_ref, w_ref, cols_ref, r1_ref, sums_ref, own_ref, other_ref, tgt_ref, fac_ref, msg_ref, edge_ref, share_ref, acc_ref
):
    tiles = w_ref.shape[1] // LANES
    factors(seg_ref, recv_ref, sums_ref, own_ref, other_ref, tgt_ref, fac_ref, edge_ref, share_ref)
    acc_ref[...] = jnp.zeros_like(acc_ref)

    def county(k, carry):
        b0, b1, c = seg_blocks(seg_ref, k)
        name = c.astype(jnp.float32)

        def block(b, inner):
            rows = rows_of(b)
            mask = cols_ref[0, rows, :] == name
            r1 = jnp.where(mask, r1_ref[rows, :], 0.0)
            sums = [None] * 4
            for t in range(tiles):
                x = w_ref[rows, tile(t)] * r1 * fac_ref[k, t : t + 1, :]
                sums[t % 4] = x if sums[t % 4] is None else sums[t % 4] + x
            acc_ref[rows, :] += (sums[0] + sums[1]) + (sums[2] + sums[3])
            return inner

        return lax.fori_loop(b0, b1, block, carry)

    lax.fori_loop(0, seg_ref[COUNT], county, 0)
    message(msg_ref, jnp.sum(acc_ref[...].T, axis=0, keepdims=True), jnp.zeros((1, LANES), jnp.float32))


def last_kernel(
    tiles_here, seg_ref, recv_ref, w_ref, cols_ref, r1_ref, r2_ref, fac_ref, sums_ref, own_ref, other_ref, tgt_ref, out_ref, fac2_ref, edge_ref, share_ref
):
    step = pl.program_id(0)

    @pl.when(step == 0)
    def _():
        factors(seg_ref, recv_ref, sums_ref, own_ref, other_ref, tgt_ref, fac2_ref, edge_ref, share_ref)

    base = step * tiles_here

    def county(k, carry):
        b0, b1, c = seg_blocks(seg_ref, k)
        name = c.astype(jnp.float32)
        one = [jnp.broadcast_to(fac_ref[k, pl.ds(base + t, 1), :], (SUB, LANES)) for t in range(tiles_here)]
        two = [jnp.broadcast_to(100.0 * fac2_ref[k, pl.ds(base + t, 1), :], (SUB, LANES)) for t in range(tiles_here)]

        def block(b, inner):
            rows = rows_of(b)
            mask = cols_ref[0, rows, :] == name
            r1 = r1_ref[rows, :]
            r2 = r2_ref[rows, :]
            for t in range(tiles_here):
                x = w_ref[rows, tile(t)] * r1 * one[t] * r2 * two[t]
                pltpu.store(out_ref.at[rows, tile(t)], x, mask=mask)
            return inner

        return lax.fori_loop(b0, b1, block, carry)

    lax.fori_loop(0, seg_ref[COUNT], county, 0)


def local(planes, parts, seed_slab, row_target, county_id, county_target):
    rows, width = seed_slab.shape
    counties = county_target.shape[0]
    tiles = width // LANES
    half_rows = tiles // 2 + 4
    cid_row = county_id.reshape(1, rows)
    goal_row = row_target.reshape(1, rows)
    block = width // CHUNKS

    def whole(*shape):
        return pl.BlockSpec(shape, lambda i: (0,) * len(shape))

    msg, seg, cols = pl.pallas_call(
        functools.partial(first_kernel, block // LANES),
        grid=(CHUNKS,),
        out_shape=(f32(parts, SUB, LANES), jax.ShapeDtypeStruct((256,), jnp.int32), f32(2, rows, LANES)),
        in_specs=[
            SMEM,
            whole(1, rows),
            whole(1, rows),
            pl.BlockSpec((rows, block), lambda i: (0, i)),
            pl.BlockSpec((counties, block), lambda i: (0, i)),
        ],
        out_specs=(whole(parts, SUB, LANES), SMEM, whole(2, rows, LANES)),
        scratch_shapes=[pltpu.VMEM((rows, LANES), jnp.float32), pltpu.VMEM((LANES, LANES), jnp.float32)],
        compiler_params=PARAMS,
        name="row_sums",
    )(county_id, cid_row, goal_row, seed_slab, county_target)

    def over_type(x):
        return lax.all_to_all(x, "type", 0, 0)

    planes_of = [[PLANE * z + s for s in range(PLANE)] for z in range(planes)]
    lines_of = [[PLANE * z + s for z in range(planes)] for s in range(PLANE)]
    pair = [(i, i ^ 1) for i in range(planes * PLANE)]

    def edges(send):
        got = lax.all_to_all(send, "bg", 0, 0, axis_index_groups=planes_of)
        out = pl.pallas_call(
            plane_kernel,
            out_shape=f32(planes, half_rows, LANES),
            in_specs=[VMEM],
            out_specs=VMEM,
            compiler_params=PARAMS,
            name="plane_sums",
        )(got)
        far = lax.all_to_all(out, "bg", 0, 0, axis_index_groups=lines_of)
        own, other = pl.pallas_call(
            edge_kernel,
            out_shape=(f32(2, half_rows, LANES), f32(2, half_rows, LANES)),
            in_specs=[VMEM, VMEM],
            out_specs=(VMEM, VMEM),
            compiler_params=PARAMS,
            name="edge_sums",
        )(got, far)
        return own, lax.ppermute(other, "bg", pair)

    sums_shapes = (f32(PLANE, 2, half_rows, LANES), f32(counties, tiles + SUB, LANES), f32(rows, LANES))
    recv1 = over_type(msg)
    send, sums, r1 = pl.pallas_call(
        functools.partial(sums_kernel, False),
        out_shape=sums_shapes,
        in_specs=[SMEM] + [VMEM] * 4,
        out_specs=(VMEM,) * 3,
        compiler_params=PARAMS,
        name="county_sums_1",
    )(seg, recv1, goal_row, seed_slab, cols)
    own, other = edges(send)
    edge_scratch = [pltpu.VMEM((2, tiles + SUB, LANES), jnp.float32), pltpu.VMEM((tiles, LANES), jnp.float32)]
    fac, msg = pl.pallas_call(
        rows_kernel,
        out_shape=(f32(counties, tiles, LANES), f32(parts, SUB, LANES)),
        in_specs=[SMEM] + [VMEM] * 8,
        out_specs=(VMEM, VMEM),
        scratch_shapes=edge_scratch + [pltpu.VMEM((rows, LANES), jnp.float32)],
        compiler_params=PARAMS,
        name="row_sums_2",
    )(seg, recv1, seed_slab, cols, r1, sums, own, other, county_target)
    recv2 = over_type(msg)
    send, sums, r2 = pl.pallas_call(
        functools.partial(sums_kernel, True),
        out_shape=sums_shapes,
        in_specs=[SMEM] + [VMEM] * 6,
        out_specs=(VMEM,) * 3,
        compiler_params=PARAMS,
        name="county_sums_2",
    )(seg, recv2, goal_row, seed_slab, cols, r1, fac)
    own, other = edges(send)
    return pl.pallas_call(
        functools.partial(last_kernel, block // LANES),
        grid=(CHUNKS,),
        out_shape=f32(rows, width),
        in_specs=[
            SMEM,
            whole(parts, SUB, LANES),
            pl.BlockSpec((rows, block), lambda i: (0, i)),
            whole(2, rows, LANES),
            whole(rows, LANES),
            whole(rows, LANES),
            whole(counties, tiles, LANES),
            whole(counties, tiles + SUB, LANES),
            whole(2, half_rows, LANES),
            whole(2, half_rows, LANES),
            whole(counties, width),
        ],
        out_specs=pl.BlockSpec((rows, block), lambda i: (0, i)),
        scratch_shapes=[pltpu.VMEM((counties, tiles, LANES), jnp.float32)] + edge_scratch,
        compiler_params=PARAMS,
        name="fitted",
    )(seg, recv1, seed_slab, cols, r1, r2, fac, sums, own, other, county_target)


def solution(mesh):
    return jax.shard_map(
        functools.partial(local, mesh.shape["bg"] // PLANE, mesh.shape["type"]),
        mesh=mesh,
        in_specs=(P("bg", "type"), P("bg"), P("bg"), P(None, "type")),
        out_specs=P("bg", "type"),
        check_vma=False,
    )
```

```python
import functools

import jax
import jax.numpy as jnp
from jax import lax
from jax.experimental import pallas as pl
from jax.experimental.pallas import tpu as pltpu
from jax.sharding import PartitionSpec as P

LANES = 128
SUB = 8
PLANE = 8
COUNT = 255
NAMES = 128
VMEM = pl.BlockSpec(memory_space=pltpu.VMEM)
SMEM = pl.BlockSpec(memory_space=pltpu.SMEM)
HBM = pl.BlockSpec(memory_space=pltpu.HBM)
PARAMS = pltpu.CompilerParams(vmem_limit_bytes=32 * 1024 * 1024)


def f32(*shape):
    return jax.ShapeDtypeStruct(shape, jnp.float32)


def tile(t):
    return pl.ds(t * LANES, LANES)


def rows_of(b):
    return pl.ds(pl.multiple_of(b * SUB, SUB), SUB)


def column(row):
    return jnp.broadcast_to(row, (LANES, LANES)).T


def fold(parts):
    sub = lax.broadcasted_iota(jnp.int32, (SUB, LANES), 0)
    order, step = list(parts), 1
    while step < SUB:
        mask = (sub & step) == 0
        merged = []
        for a, b in zip(order[0::2], order[1::2]):
            merged.append(jnp.where(mask, a, b) + pltpu.roll(jnp.where(mask, b, a), SUB - step, 0))
        order, step = merged, 2 * step
    return order[0]


def seg_blocks(seg_ref, k):
    first = seg_ref[k]
    end = seg_ref[k + 1]
    return first >> 3, (end + 7) >> 3, seg_ref[NAMES + k]


def message(msg_ref, row_sum, share):
    sub = lax.broadcasted_iota(jnp.int32, (SUB, LANES), 0)
    msg_ref[...] = jnp.where(sub == 0, row_sum, jnp.where(sub == 1, share, 0.0))


def first_kernel(
    chunks, cid_hbm, cid_row_hbm, goal_row_hbm, w_hbm, tgt_hbm, msg_ref, seg_ref, cols_ref, w_ref, share_ref, cid_ref, cid_row, goal_row, tgt_ref, acc_w, acc_t, sems
):
    rows, width = w_ref.shape
    counties = tgt_ref.shape[0]
    tiles = width // LANES
    block = width // chunks
    small = [
        pltpu.make_async_copy(cid_hbm, cid_ref, sems.at[0]),
        pltpu.make_async_copy(cid_row_hbm, cid_row, sems.at[1]),
        pltpu.make_async_copy(goal_row_hbm, goal_row, sems.at[2]),
    ]
    targets = pltpu.make_async_copy(tgt_hbm, tgt_ref, sems.at[3])
    slabs = []
    for q in range(chunks):
        part = pl.ds(q * block, block)
        slabs.append(pltpu.make_async_copy(w_hbm.at[:, part], w_ref.at[:, part], sems.at[4 + q]))
    for copy in small + [targets] + slabs:
        copy.start()
    for copy in small:
        copy.wait()

    n = jnp.int32(0)
    seg_ref[0] = 0
    for g in range(rows):
        c = cid_ref[g]
        seg_ref[NAMES + n] = c
        seg_ref[n + 1] = g + 1
        if g + 1 < rows:
            n = n + (cid_ref[g + 1] != c).astype(jnp.int32)
    n = n + 1
    seg_ref[COUNT] = n
    cols_ref[0] = column(cid_row[...].astype(jnp.float32))
    cols_ref[1] = column(goal_row[...].astype(jnp.float32))
    acc_w[...] = jnp.zeros_like(acc_w)
    acc_t[...] = jnp.zeros_like(acc_t)

    targets.wait()

    @pl.loop(0, counties // SUB)
    def _(b):
        part = rows_of(b)
        accs = [jnp.zeros((SUB, LANES), jnp.float32)] * 4
        for t in range(tiles):
            accs[t % 4] = accs[t % 4] + tgt_ref[part, tile(t)].astype(jnp.float32)
        acc_t[part, :] = (accs[0] + accs[1]) + (accs[2] + accs[3])

    sub = lax.broadcasted_iota(jnp.int32, (SUB, LANES), 0)

    @pl.loop(0, n)
    def _(k):
        c = seg_ref[NAMES + k]
        part = rows_of(c >> 3)
        mask = sub == (c & 7)
        for t in range(0, tiles, SUB):
            parts = [jnp.where(mask, tgt_ref[part, tile(t + i)].astype(jnp.float32), 0.0) for i in range(SUB)]
            share_ref[k, t : t + SUB, :] = fold(parts)

    for q in range(chunks):
        slabs[q].wait()

        @pl.loop(0, rows // SUB)
        def _(b):
            part = rows_of(b)
            accs = [acc_w[part, :]] + [jnp.zeros((SUB, LANES), jnp.float32)] * 3
            for i in range(block // LANES):
                accs[i % 4] = accs[i % 4] + w_ref[part, tile(q * (block // LANES) + i)]
            acc_w[part, :] = (accs[0] + accs[1]) + (accs[2] + accs[3])

    row_sum = jnp.sum(acc_w[...].T, axis=0, keepdims=True)
    share = jnp.sum(acc_t[...].T, axis=0, keepdims=True)
    message(msg_ref, row_sum, share)


def sums_kernel(second, parts_n, *refs):
    seg_ref, refs = refs[0], refs[1:]
    msgs, refs = refs[:parts_n], refs[parts_n:]
    if second:
        w_ref, cols_ref, r1_ref, fac_ref, keep_ref, give_ref, sums_ref, rcol_ref, total_ref = refs
        chunks = 3
    else:
        w_ref, cols_ref, keep_ref, give_ref, sums_ref, rcol_ref, total_ref = refs
        chunks = 2
    tiles = w_ref.shape[1] // LANES
    half = tiles // 2
    width = tiles // chunks
    total = msgs[0][...]
    for m in msgs[1:]:
        total = total + m[...]
    total_ref[...] = total
    rcol_ref[...] = cols_ref[1] / column(total[0:1])
    n = seg_ref[COUNT]
    sub = lax.broadcasted_iota(jnp.int32, (SUB, LANES), 0)

    def county(k, carry):
        b0, b1, c = seg_blocks(seg_ref, k)
        name = c.astype(jnp.float32)
        if second:
            people = jnp.zeros((1, LANES), jnp.float32)
        else:

            def persons(b, acc):
                rows = rows_of(b)
                return acc + jnp.where(cols_ref[0, rows, :] == name, cols_ref[1, rows, :], 0.0)

            people = lax.fori_loop(b0, b1, persons, jnp.zeros((SUB, LANES), jnp.float32))
            people = jnp.sum(people, axis=0, keepdims=True)
        sums_ref[k, tiles : tiles + SUB, :] = jnp.where(sub == 0, people, jnp.where(sub == 1, name, 0.0))
        parts = []
        for q in range(chunks):
            own = range(q * width, (q + 1) * width)
            if second:
                factor = [jnp.broadcast_to(fac_ref[k, t : t + 1, :], (SUB, LANES)) for t in own]

            def block(b, accs):
                rows = rows_of(b)
                mask = cols_ref[0, rows, :] == name
                out = []
                if second:
                    r1 = jnp.where(mask, r1_ref[rows, :], 0.0)
                    r2 = rcol_ref[rows, :]
                    for i, t in enumerate(own):
                        out.append(accs[i] + w_ref[rows, tile(t)] * r1 * factor[i] * r2)
                else:
                    r1 = jnp.where(mask, rcol_ref[rows, :], 0.0)
                    for i, t in enumerate(own):
                        out.append(accs[i] + w_ref[rows, tile(t)] * r1)
                return tuple(out)

            parts.extend(lax.fori_loop(b0, b1, block, tuple(jnp.zeros((SUB, LANES), jnp.float32) for _ in own)))
            while len(parts) >= SUB:
                at = (q + 1) * width - len(parts)
                sums_ref[k, at : at + SUB, :] = fold(parts[:SUB])
                parts = parts[SUB:]
        return carry

    lax.fori_loop(0, n, county, 0)
    core = lax.axis_index("bg") % 2
    for mine in range(2):

        @pl.when(core == mine)
        def _():
            for out_ref, h in ((keep_ref, mine), (give_ref, 1 - mine)):
                for e, k in ((0, 0), (1, n - 1)):
                    out_ref[e, 0:half, :] = sums_ref[k, h * half : (h + 1) * half, :]
                    out_ref[e, half : half + 4, :] = sums_ref[k, tiles : tiles + 4, :]


def join(refs):
    rows = refs[0].shape[1]
    name = rows - 3
    sub = lax.broadcasted_iota(jnp.int32, (rows, LANES), 0)
    out = []
    for e, pick in ((0, jnp.minimum), (1, jnp.maximum)):
        names = [ref[e, name : name + 1, :] for ref in refs]
        edge = functools.reduce(pick, names)
        total = jnp.zeros((rows, LANES), jnp.float32)
        for ref, own in zip(refs, names):
            total = total + jnp.where(own == edge, ref[e], 0.0)
        out.append(jnp.where(sub == name, edge, total))
    return out


def chip_kernel(keep_ref, got_ref, chip_ref):
    head, tail = join([keep_ref, got_ref])
    chip_ref[0] = head
    chip_ref[1] = tail


def plane_kernel(*refs):
    send_ref = refs[-1]
    z = lax.axis_index("bg") // PLANE
    head, tail = join(refs[:-1])
    for j in range(send_ref.shape[0]):

        @pl.when(j > z)
        def _():
            send_ref[j] = tail

        @pl.when(j <= z)
        def _():
            send_ref[j] = head


def edge_kernel(keep_ref, got_ref, far_ref, *refs):
    chips, (own_ref, other_ref) = refs[:-2], refs[-2:]
    planes, rows = far_ref.shape[:2]
    me = lax.axis_index("bg")
    z = me // PLANE
    x = (me // 2) % (PLANE // 2)
    core = me % 2
    name = rows - 3
    sub = lax.broadcasted_iota(jnp.int32, (rows, LANES), 0)

    for mine_ref, near_ref, out_ref, side in ((keep_ref, got_ref, own_ref, core), (got_ref, keep_ref, other_ref, 1 - core)):
        for e in range(2):
            county = mine_ref[e, name : name + 1, :]
            total = mine_ref[e]

            def add(total, ref, county=county):
                return total + jnp.where(ref[name : name + 1, :] == county, ref[...], 0.0)

            total = add(total, near_ref.at[side])
            for m, chip_ref in enumerate(chips, 1):
                total = add(total, chip_ref.at[jnp.where((x ^ m) < x, 1, 0)])
            for j in range(planes):
                hit = jnp.logical_and(far_ref[j, name : name + 1, :] == county, j != z)
                total = total + jnp.where(hit, far_ref[j], 0.0)
            out_ref[e] = total


def edges_of(tiles, own_ref, other_ref, edge_ref):
    half = tiles // 2
    core = lax.axis_index("bg") % 2
    for mine, left_ref, right_ref in ((0, own_ref, other_ref), (1, other_ref, own_ref)):

        @pl.when(core == mine)
        def _():
            for e in range(2):
                edge_ref[e, 0:half, :] = left_ref[e, 0:half, :]
                edge_ref[e, half:tiles, :] = right_ref[e, 0:half, :]
                edge_ref[e, tiles : tiles + 4, :] = left_ref[e, half : half + 4, :]


def rows_kernel(
    seg_ref, total_ref, w_ref, cols_ref, r1_ref, sums_ref, own_ref, other_ref, share_ref, fac_ref, goal_ref, msg_ref, edge_ref, acc_ref
):
    tiles = w_ref.shape[1] // LANES
    n = seg_ref[COUNT]
    edges_of(tiles, own_ref, other_ref, edge_ref)
    share = total_ref[1:2, :]
    lane = lax.broadcasted_iota(jnp.int32, (1, LANES), 1)

    def factor(k, sum_ref):
        whole = jnp.sum(jnp.where(lane == seg_ref[NAMES + k], share, 0.0), axis=1, keepdims=True)
        goal = share_ref[k] * (sum_ref[tiles : tiles + 1, :] / whole)
        goal_ref[k] = goal
        fac_ref[k] = goal / sum_ref[0:tiles, :]

    factor(0, edge_ref.at[0])
    factor(n - 1, edge_ref.at[1])

    @pl.loop(1, n - 1)
    def _(k):
        factor(k, sums_ref.at[k])

    acc_ref[...] = jnp.zeros_like(acc_ref)

    def county(k, carry):
        b0, b1, c = seg_blocks(seg_ref, k)
        name = c.astype(jnp.float32)

        def block(b, inner):
            rows = rows_of(b)
            mask = cols_ref[0, rows, :] == name
            r1 = jnp.where(mask, r1_ref[rows, :], 0.0)
            sums = [None] * 4
            for t in range(tiles):
                x = w_ref[rows, tile(t)] * r1 * fac_ref[k, t : t + 1, :]
                sums[t % 4] = x if sums[t % 4] is None else sums[t % 4] + x
            acc_ref[rows, :] += (sums[0] + sums[1]) + (sums[2] + sums[3])
            return inner

        return lax.fori_loop(b0, b1, block, carry)

    lax.fori_loop(0, n, county, 0)
    message(msg_ref, jnp.sum(acc_ref[...].T, axis=0, keepdims=True), jnp.zeros((1, LANES), jnp.float32))


def last_kernel(
    chunks, seg_ref, w_ref, cols_ref, r1_ref, r2_ref, fac_ref, goal_ref, sums_ref, own_ref, other_ref, out_hbm, out_ref, fac2_ref, edge_ref, sems
):
    width = w_ref.shape[1]
    tiles = width // LANES
    here = tiles // chunks
    n = seg_ref[COUNT]
    edges_of(tiles, own_ref, other_ref, edge_ref)
    fac2_ref[0] = goal_ref[0] / edge_ref[0, 0:tiles, :]
    fac2_ref[n - 1] = goal_ref[n - 1] / edge_ref[1, 0:tiles, :]

    @pl.loop(1, n - 1)
    def _(k):
        fac2_ref[k] = goal_ref[k] / sums_ref[k, 0:tiles, :]

    copies = []
    for q in range(chunks):
        own = range(q * here, (q + 1) * here)

        def county(k, carry):
            b0, b1, c = seg_blocks(seg_ref, k)
            name = c.astype(jnp.float32)
            one = [jnp.broadcast_to(fac_ref[k, t : t + 1, :], (SUB, LANES)) for t in own]
            two = [jnp.broadcast_to(fac2_ref[k, t : t + 1, :], (SUB, LANES)) for t in own]

            def block(b, inner):
                rows = rows_of(b)
                mask = cols_ref[0, rows, :] == name
                r1 = r1_ref[rows, :]
                r2 = r2_ref[rows, :]
                for i, t in enumerate(own):
                    x = w_ref[rows, tile(t)] * r1 * one[i] * r2 * two[i] * 100.0
                    pltpu.store(out_ref.at[rows, tile(t)], x, mask=mask)
                return inner

            return lax.fori_loop(b0, b1, block, carry)

        lax.fori_loop(0, n, county, 0)
        part = pl.ds(q * here * LANES, here * LANES)
        copy = pltpu.make_async_copy(out_ref.at[:, part], out_hbm.at[:, part], sems.at[q])
        copy.start()
        copies.append(copy)
    for copy in copies:
        copy.wait()


def call(kernel, name, ins, in_specs, out_shape, out_specs=None, scratch=()):
    if out_specs is None:
        out_specs = jax.tree.map(lambda _: VMEM, out_shape)
    return pl.pallas_call(
        kernel, out_shape=out_shape, in_specs=in_specs, out_specs=out_specs, scratch_shapes=scratch, compiler_params=PARAMS, name=name
    )(*ins)


def local(planes, parts, seed_slab, row_target, county_id, county_target):
    rows, width = seed_slab.shape
    counties = county_target.shape[0]
    tiles = width // LANES
    half_rows = tiles // 2 + 4
    in_chunks, out_chunks = 8, 4
    device = planes * PLANE

    edge = f32(2, half_rows, LANES)
    table = f32(counties, tiles, LANES)
    column_of = f32(rows, LANES)
    small = f32(SUB, LANES)
    msg, seg, cols, slab, share = call(
        functools.partial(first_kernel, in_chunks),
        "row_sums_1",
        (county_id, county_id.reshape(1, rows), row_target.reshape(1, rows), seed_slab, county_target),
        [HBM] * 5,
        (small, jax.ShapeDtypeStruct((256,), jnp.int32), f32(2, rows, LANES), f32(rows, width), table),
        (VMEM, SMEM, VMEM, VMEM, VMEM),
        [
            pltpu.SMEM((rows,), jnp.int32),
            pltpu.VMEM((1, rows), jnp.int32),
            pltpu.VMEM((1, rows), jnp.int32),
            pltpu.VMEM((counties, width), jnp.int32),
            pltpu.VMEM((rows, LANES), jnp.float32),
            pltpu.VMEM((LANES, LANES), jnp.float32),
            pltpu.SemaphoreType.DMA((4 + in_chunks,)),
        ],
    )

    def swap(x, axis, size, mask):
        return lax.ppermute(x, axis, [(i, i ^ mask) for i in range(size)])

    def over_type(x):
        return [x] + [swap(x, "type", parts, m) for m in range(1, parts)]

    lines = [[PLANE * z + s for z in range(planes)] for s in range(PLANE)]

    def edges(keep, give):
        got = swap(give, "bg", device, 1)
        chip = call(chip_kernel, "chip_sums", (keep, got), [VMEM] * 2, edge)
        chips = [swap(chip, "bg", device, 2 * m) for m in range(1, PLANE // 2)]
        send = call(plane_kernel, "plane_sums", [chip] + chips, [VMEM] * (PLANE // 2), f32(planes, half_rows, LANES))
        far = lax.all_to_all(send, "bg", 0, 0, axis_index_groups=lines)
        own, other = call(edge_kernel, "edge_sums", [keep, got, far] + chips, [VMEM] * (2 + PLANE // 2), (edge, edge))
        return own, swap(other, "bg", device, 1)

    sums_shapes = (edge, edge, f32(counties, tiles + SUB, LANES), column_of, small)
    edge_scratch = pltpu.VMEM((2, tiles + SUB, LANES), jnp.float32)
    keep, give, sums, r1, total = call(
        functools.partial(sums_kernel, False, parts),
        "county_sums_1",
        [seg] + over_type(msg) + [slab, cols],
        [SMEM] + [VMEM] * (parts + 2),
        sums_shapes,
    )
    own, other = edges(keep, give)
    fac, goal, msg = call(
        rows_kernel,
        "row_sums_2",
        (seg, total, slab, cols, r1, sums, own, other, share),
        [SMEM] + [VMEM] * 8,
        (table, table, small),
        None,
        [edge_scratch, pltpu.VMEM((rows, LANES), jnp.float32)],
    )
    keep, give, sums, r2, _ = call(
        functools.partial(sums_kernel, True, parts),
        "county_sums_2",
        [seg] + over_type(msg) + [slab, cols, r1, fac],
        [SMEM] + [VMEM] * (parts + 4),
        sums_shapes,
    )
    own, other = edges(keep, give)
    return call(
        functools.partial(last_kernel, out_chunks),
        "fitted",
        (seg, slab, cols, r1, r2, fac, goal, sums, own, other),
        [SMEM] + [VMEM] * 9,
        f32(rows, width),
        HBM,
        [
            pltpu.VMEM((rows, width), jnp.float32),
            pltpu.VMEM((counties, tiles, LANES), jnp.float32),
            edge_scratch,
            pltpu.SemaphoreType.DMA((out_chunks,)),
        ],
    )


def solution(mesh):
    return jax.shard_map(
        functools.partial(local, mesh.shape["bg"] // PLANE, mesh.shape["type"]),
        mesh=mesh,
        in_specs=(P("bg", "type"), P("bg"), P("bg"), P(None, "type")),
        out_specs=P("bg", "type"),
        check_vma=False,
    )
```

```python
import functools

import jax
import jax.numpy as jnp
from jax import lax
from jax.experimental import pallas as pl
from jax.experimental.pallas import tpu as pltpu
from jax.sharding import PartitionSpec as P

LANES = 128
SUB = 8
PLANE = 8
COUNT = 255
NAMES = 128
VMEM = pl.BlockSpec(memory_space=pltpu.VMEM)
SMEM = pl.BlockSpec(memory_space=pltpu.SMEM)
HBM = pl.BlockSpec(memory_space=pltpu.HBM)
PARAMS = pltpu.CompilerParams(vmem_limit_bytes=32 * 1024 * 1024)


def f32(*shape):
    return jax.ShapeDtypeStruct(shape, jnp.float32)


def tile(t):
    return pl.ds(t * LANES, LANES)


def rows_of(b):
    return pl.ds(pl.multiple_of(b * SUB, SUB), SUB)


def column(row):
    return jnp.broadcast_to(row, (LANES, LANES)).T


def fold(parts):
    sub = lax.broadcasted_iota(jnp.int32, (SUB, LANES), 0)
    order, step = list(parts), 1
    while step < SUB:
        mask = (sub & step) == 0
        merged = []
        for a, b in zip(order[0::2], order[1::2]):
            merged.append(jnp.where(mask, a, b) + pltpu.roll(jnp.where(mask, b, a), SUB - step, 0))
        order, step = merged, 2 * step
    return order[0]


def seg_blocks(seg_ref, k):
    first = seg_ref[k]
    end = seg_ref[k + 1]
    return first >> 3, (end + 7) >> 3, seg_ref[NAMES + k]


def message(msg_ref, row_sum, share):
    sub = lax.broadcasted_iota(jnp.int32, (SUB, LANES), 0)
    msg_ref[...] = jnp.where(sub == 0, row_sum, jnp.where(sub == 1, share, 0.0))


def first_kernel(
    chunks, cid_hbm, cid_row_hbm, goal_row_hbm, w_hbm, tgt_hbm, msg_ref, seg_ref, cols_ref, w_ref, share_ref, cid_ref, cid_row, goal_row, tgt_ref, acc_w, acc_t, sems
):
    rows, width = w_ref.shape
    counties = tgt_ref.shape[0]
    tiles = width // LANES
    block = width // chunks
    small = [
        pltpu.make_async_copy(cid_hbm, cid_ref, sems.at[0]),
        pltpu.make_async_copy(cid_row_hbm, cid_row, sems.at[1]),
        pltpu.make_async_copy(goal_row_hbm, goal_row, sems.at[2]),
    ]
    targets = pltpu.make_async_copy(tgt_hbm, tgt_ref, sems.at[3])
    slabs = []
    for q in range(chunks):
        part = pl.ds(q * block, block)
        slabs.append(pltpu.make_async_copy(w_hbm.at[:, part], w_ref.at[:, part], sems.at[4 + q]))
    for copy in small + [targets] + slabs:
        copy.start()
    for copy in small:
        copy.wait()

    n = jnp.int32(0)
    seg_ref[0] = 0
    for g in range(rows):
        c = cid_ref[g]
        seg_ref[NAMES + n] = c
        seg_ref[n + 1] = g + 1
        if g + 1 < rows:
            n = n + (cid_ref[g + 1] != c).astype(jnp.int32)
    n = n + 1
    seg_ref[COUNT] = n
    cols_ref[0] = column(cid_row[...].astype(jnp.float32))
    cols_ref[1] = column(goal_row[...].astype(jnp.float32))
    acc_w[...] = jnp.zeros_like(acc_w)
    acc_t[...] = jnp.zeros_like(acc_t)

    targets.wait()

    @pl.loop(0, counties // SUB)
    def _(b):
        part = rows_of(b)
        accs = [jnp.zeros((SUB, LANES), jnp.float32)] * 4
        for t in range(tiles):
            accs[t % 4] = accs[t % 4] + tgt_ref[part, tile(t)].astype(jnp.float32)
        acc_t[part, :] = (accs[0] + accs[1]) + (accs[2] + accs[3])

    sub = lax.broadcasted_iota(jnp.int32, (SUB, LANES), 0)

    @pl.loop(0, n)
    def _(k):
        c = seg_ref[NAMES + k]
        part = rows_of(c >> 3)
        mask = sub == (c & 7)
        for t in range(0, tiles, SUB):
            parts = [jnp.where(mask, tgt_ref[part, tile(t + i)].astype(jnp.float32), 0.0) for i in range(SUB)]
            share_ref[k, t : t + SUB, :] = fold(parts)

    for q in range(chunks):
        slabs[q].wait()

        @pl.loop(0, rows // SUB)
        def _(b):
            part = rows_of(b)
            accs = [acc_w[part, :]] + [jnp.zeros((SUB, LANES), jnp.float32)] * 3
            for i in range(block // LANES):
                accs[i % 4] = accs[i % 4] + w_ref[part, tile(q * (block // LANES) + i)]
            acc_w[part, :] = (accs[0] + accs[1]) + (accs[2] + accs[3])

    row_sum = jnp.sum(acc_w[...].T, axis=0, keepdims=True)
    share = jnp.sum(acc_t[...].T, axis=0, keepdims=True)
    message(msg_ref, row_sum, share)


def sums_kernel(second, parts_n, *refs):
    seg_ref, refs = refs[0], refs[1:]
    msgs, refs = refs[:parts_n], refs[parts_n:]
    if second:
        w_ref, cols_ref, r1_ref, fac_ref, keep_ref, give_ref, sums_ref, rcol_ref, total_ref = refs
        chunks = 4
    else:
        w_ref, cols_ref, keep_ref, give_ref, sums_ref, rcol_ref, total_ref = refs
        chunks = 2
    tiles = w_ref.shape[1] // LANES
    half = tiles // 2
    width = tiles // chunks
    total = msgs[0][...]
    for m in msgs[1:]:
        total = total + m[...]
    total_ref[...] = total
    rcol_ref[...] = cols_ref[1] / column(total[0:1])
    n = seg_ref[COUNT]
    sub = lax.broadcasted_iota(jnp.int32, (SUB, LANES), 0)

    def county(k, carry):
        b0, b1, c = seg_blocks(seg_ref, k)
        name = c.astype(jnp.float32)
        if second:
            people = jnp.zeros((1, LANES), jnp.float32)
        else:

            def persons(b, acc):
                rows = rows_of(b)
                return acc + jnp.where(cols_ref[0, rows, :] == name, cols_ref[1, rows, :], 0.0)

            people = lax.fori_loop(b0, b1, persons, jnp.zeros((SUB, LANES), jnp.float32))
            people = jnp.sum(people, axis=0, keepdims=True)
        sums_ref[k, tiles : tiles + SUB, :] = jnp.where(sub == 0, people, jnp.where(sub == 1, name, 0.0))
        parts = []
        for q in range(chunks):
            own = range(q * width, (q + 1) * width)
            if second:
                factor = [jnp.broadcast_to(fac_ref[k, t : t + 1, :], (SUB, LANES)) for t in own]

            def block(b, accs):
                rows = rows_of(b)
                mask = cols_ref[0, rows, :] == name
                out = []
                if second:
                    r1 = jnp.where(mask, r1_ref[rows, :], 0.0)
                    r2 = rcol_ref[rows, :]
                    for i, t in enumerate(own):
                        out.append(accs[i] + w_ref[rows, tile(t)] * r1 * factor[i] * r2)
                else:
                    r1 = jnp.where(mask, rcol_ref[rows, :], 0.0)
                    for i, t in enumerate(own):
                        out.append(accs[i] + w_ref[rows, tile(t)] * r1)
                return tuple(out)

            parts.extend(lax.fori_loop(b0, b1, block, tuple(jnp.zeros((SUB, LANES), jnp.float32) for _ in own)))
            while len(parts) >= SUB:
                at = (q + 1) * width - len(parts)
                sums_ref[k, at : at + SUB, :] = fold(parts[:SUB])
                parts = parts[SUB:]
        return carry

    lax.fori_loop(0, n, county, 0)
    core = lax.axis_index("bg") % 2
    for mine in range(2):

        @pl.when(core == mine)
        def _():
            for out_ref, h in ((keep_ref, mine), (give_ref, 1 - mine)):
                for e, k in ((0, 0), (1, n - 1)):
                    out_ref[e, 0:half, :] = sums_ref[k, h * half : (h + 1) * half, :]
                    out_ref[e, half : half + 4, :] = sums_ref[k, tiles : tiles + 4, :]


def join(refs):
    rows = refs[0].shape[1]
    name = rows - 3
    sub = lax.broadcasted_iota(jnp.int32, (rows, LANES), 0)
    out = []
    for e, pick in ((0, jnp.minimum), (1, jnp.maximum)):
        names = [ref[e, name : name + 1, :] for ref in refs]
        edge = functools.reduce(pick, names)
        total = jnp.zeros((rows, LANES), jnp.float32)
        for ref, own in zip(refs, names):
            total = total + jnp.where(own == edge, ref[e], 0.0)
        out.append(jnp.where(sub == name, edge, total))
    return out


def chip_kernel(keep_ref, got_ref, chip_ref):
    head, tail = join([keep_ref, got_ref])
    chip_ref[0] = head
    chip_ref[1] = tail


def plane_kernel(*refs):
    send_ref = refs[-1]
    z = lax.axis_index("bg") // PLANE
    head, tail = join(refs[:-1])
    for j in range(send_ref.shape[0]):

        @pl.when(j > z)
        def _():
            send_ref[j] = tail

        @pl.when(j <= z)
        def _():
            send_ref[j] = head


def edge_kernel(keep_ref, got_ref, far_ref, *refs):
    chips, (own_ref, other_ref) = refs[:-2], refs[-2:]
    planes, rows = far_ref.shape[:2]
    me = lax.axis_index("bg")
    z = me // PLANE
    x = (me // 2) % (PLANE // 2)
    core = me % 2
    name = rows - 3
    sub = lax.broadcasted_iota(jnp.int32, (rows, LANES), 0)

    for mine_ref, near_ref, out_ref, side in ((keep_ref, got_ref, own_ref, core), (got_ref, keep_ref, other_ref, 1 - core)):
        for e in range(2):
            county = mine_ref[e, name : name + 1, :]
            total = mine_ref[e]

            def add(total, ref, county=county):
                return total + jnp.where(ref[name : name + 1, :] == county, ref[...], 0.0)

            total = add(total, near_ref.at[side])
            for m, chip_ref in enumerate(chips, 1):
                total = add(total, chip_ref.at[jnp.where((x ^ m) < x, 1, 0)])
            for j in range(planes):
                hit = jnp.logical_and(far_ref[j, name : name + 1, :] == county, j != z)
                total = total + jnp.where(hit, far_ref[j], 0.0)
            out_ref[e] = total


def edges_of(tiles, own_ref, other_ref, edge_ref):
    half = tiles // 2
    core = lax.axis_index("bg") % 2
    for mine, left_ref, right_ref in ((0, own_ref, other_ref), (1, other_ref, own_ref)):

        @pl.when(core == mine)
        def _():
            for e in range(2):
                edge_ref[e, 0:half, :] = left_ref[e, 0:half, :]
                edge_ref[e, half:tiles, :] = right_ref[e, 0:half, :]
                edge_ref[e, tiles : tiles + 4, :] = left_ref[e, half : half + 4, :]


def rows_kernel(
    seg_ref, total_ref, w_ref, cols_ref, r1_ref, sums_ref, own_ref, other_ref, share_ref, fac_ref, goal_ref, msg_ref, edge_ref, acc_ref
):
    tiles = w_ref.shape[1] // LANES
    n = seg_ref[COUNT]
    edges_of(tiles, own_ref, other_ref, edge_ref)
    share = total_ref[1:2, :]
    lane = lax.broadcasted_iota(jnp.int32, (1, LANES), 1)

    def factor(k, sum_ref):
        whole = jnp.sum(jnp.where(lane == seg_ref[NAMES + k], share, 0.0), axis=1, keepdims=True)
        goal = share_ref[k] * (sum_ref[tiles : tiles + 1, :] / whole)
        goal_ref[k] = goal
        fac_ref[k] = goal / sum_ref[0:tiles, :]

    factor(0, edge_ref.at[0])
    factor(n - 1, edge_ref.at[1])

    @pl.loop(1, n - 1)
    def _(k):
        factor(k, sums_ref.at[k])

    acc_ref[...] = jnp.zeros_like(acc_ref)

    def county(k, carry):
        b0, b1, c = seg_blocks(seg_ref, k)
        name = c.astype(jnp.float32)

        def block(b, inner):
            rows = rows_of(b)
            mask = cols_ref[0, rows, :] == name
            r1 = jnp.where(mask, r1_ref[rows, :], 0.0)
            sums = [None] * 4
            for t in range(tiles):
                x = w_ref[rows, tile(t)] * r1 * fac_ref[k, t : t + 1, :]
                sums[t % 4] = x if sums[t % 4] is None else sums[t % 4] + x
            acc_ref[rows, :] += (sums[0] + sums[1]) + (sums[2] + sums[3])
            return inner

        return lax.fori_loop(b0, b1, block, carry)

    lax.fori_loop(0, n, county, 0)
    message(msg_ref, jnp.sum(acc_ref[...].T, axis=0, keepdims=True), jnp.zeros((1, LANES), jnp.float32))


def last_kernel(
    chunks, seg_ref, w_ref, cols_ref, r1_ref, r2_ref, fac_ref, goal_ref, sums_ref, own_ref, other_ref, out_hbm, out_ref, fac2_ref, edge_ref, sems
):
    width = w_ref.shape[1]
    tiles = width // LANES
    here = tiles // chunks
    n = seg_ref[COUNT]
    edges_of(tiles, own_ref, other_ref, edge_ref)
    fac2_ref[0] = goal_ref[0] / edge_ref[0, 0:tiles, :]
    fac2_ref[n - 1] = goal_ref[n - 1] / edge_ref[1, 0:tiles, :]

    @pl.loop(1, n - 1)
    def _(k):
        fac2_ref[k] = goal_ref[k] / sums_ref[k, 0:tiles, :]

    copies = []
    for q in range(chunks):
        own = range(q * here, (q + 1) * here)

        def county(k, carry):
            b0, b1, c = seg_blocks(seg_ref, k)
            name = c.astype(jnp.float32)
            one = [jnp.broadcast_to(fac_ref[k, t : t + 1, :], (SUB, LANES)) for t in own]
            two = [jnp.broadcast_to(fac2_ref[k, t : t + 1, :], (SUB, LANES)) for t in own]

            def block(b, inner):
                rows = rows_of(b)
                mask = cols_ref[0, rows, :] == name
                r1 = r1_ref[rows, :]
                r2 = r2_ref[rows, :]
                for i, t in enumerate(own):
                    x = w_ref[rows, tile(t)] * r1 * one[i] * r2 * two[i] * 100.0
                    pltpu.store(out_ref.at[rows, tile(t)], x, mask=mask)
                return inner

            return lax.fori_loop(b0, b1, block, carry)

        lax.fori_loop(0, n, county, 0)
        part = pl.ds(q * here * LANES, here * LANES)
        copy = pltpu.make_async_copy(out_ref.at[:, part], out_hbm.at[:, part], sems.at[q])
        copy.start()
        copies.append(copy)
    for copy in copies:
        copy.wait()


def call(kernel, name, ins, in_specs, out_shape, out_specs=None, scratch=()):
    if out_specs is None:
        out_specs = jax.tree.map(lambda _: VMEM, out_shape)
    return pl.pallas_call(
        kernel, out_shape=out_shape, in_specs=in_specs, out_specs=out_specs, scratch_shapes=scratch, compiler_params=PARAMS, name=name
    )(*ins)


def local(planes, parts, seed_slab, row_target, county_id, county_target):
    rows, width = seed_slab.shape
    counties = county_target.shape[0]
    tiles = width // LANES
    half_rows = tiles // 2 + 4
    in_chunks, out_chunks = 8, 4
    device = planes * PLANE

    edge = f32(2, half_rows, LANES)
    table = f32(counties, tiles, LANES)
    column_of = f32(rows, LANES)
    small = f32(SUB, LANES)
    msg, seg, cols, slab, share = call(
        functools.partial(first_kernel, in_chunks),
        "row_sums_1",
        [
            pltpu.with_memory_space_constraint(x, pltpu.HBM)
            for x in (county_id, county_id.reshape(1, rows), row_target.reshape(1, rows), seed_slab, county_target)
        ],
        [HBM] * 5,
        (small, jax.ShapeDtypeStruct((256,), jnp.int32), f32(2, rows, LANES), f32(rows, width), table),
        (VMEM, SMEM, VMEM, VMEM, VMEM),
        [
            pltpu.SMEM((rows,), jnp.int32),
            pltpu.VMEM((1, rows), jnp.int32),
            pltpu.VMEM((1, rows), jnp.int32),
            pltpu.VMEM((counties, width), jnp.int32),
            pltpu.VMEM((rows, LANES), jnp.float32),
            pltpu.VMEM((LANES, LANES), jnp.float32),
            pltpu.SemaphoreType.DMA((4 + in_chunks,)),
        ],
    )

    def swap(x, axis, size, mask):
        return lax.ppermute(x, axis, [(i, i ^ mask) for i in range(size)])

    def over_type(x):
        return [x] + [swap(x, "type", parts, m) for m in range(1, parts)]

    lines = [[PLANE * z + s for z in range(planes)] for s in range(PLANE)]

    def edges(keep, give):
        got = swap(give, "bg", device, 1)
        chip = call(chip_kernel, "chip_sums", (keep, got), [VMEM] * 2, edge)
        chips = [swap(chip, "bg", device, 2 * m) for m in range(1, PLANE // 2)]
        send = call(plane_kernel, "plane_sums", [chip] + chips, [VMEM] * (PLANE // 2), f32(planes, half_rows, LANES))
        far = lax.all_to_all(send, "bg", 0, 0, axis_index_groups=lines)
        own, other = call(edge_kernel, "edge_sums", [keep, got, far] + chips, [VMEM] * (2 + PLANE // 2), (edge, edge))
        return own, swap(other, "bg", device, 1)

    sums_shapes = (edge, edge, f32(counties, tiles + SUB, LANES), column_of, small)
    edge_scratch = pltpu.VMEM((2, tiles + SUB, LANES), jnp.float32)
    keep, give, sums, r1, total = call(
        functools.partial(sums_kernel, False, parts),
        "county_sums_1",
        [seg] + over_type(msg) + [slab, cols],
        [SMEM] + [VMEM] * (parts + 2),
        sums_shapes,
    )
    own, other = edges(keep, give)
    fac, goal, msg = call(
        rows_kernel,
        "row_sums_2",
        (seg, total, slab, cols, r1, sums, own, other, share),
        [SMEM] + [VMEM] * 8,
        (table, table, small),
        None,
        [edge_scratch, pltpu.VMEM((rows, LANES), jnp.float32)],
    )
    keep, give, sums, r2, _ = call(
        functools.partial(sums_kernel, True, parts),
        "county_sums_2",
        [seg] + over_type(msg) + [slab, cols, r1, fac],
        [SMEM] + [VMEM] * (parts + 4),
        sums_shapes,
    )
    own, other = edges(keep, give)
    return call(
        functools.partial(last_kernel, out_chunks),
        "fitted",
        (seg, slab, cols, r1, r2, fac, goal, sums, own, other),
        [SMEM] + [VMEM] * 9,
        f32(rows, width),
        HBM,
        [
            pltpu.VMEM((rows, width), jnp.float32),
            pltpu.VMEM((counties, tiles, LANES), jnp.float32),
            edge_scratch,
            pltpu.SemaphoreType.DMA((out_chunks,)),
        ],
    )


def solution(mesh):
    return jax.shard_map(
        functools.partial(local, mesh.shape["bg"] // PLANE, mesh.shape["type"]),
        mesh=mesh,
        in_specs=(P("bg", "type"), P("bg"), P("bg"), P(None, "type")),
        out_specs=P("bg", "type"),
        check_vma=False,
    )
```

```python
import functools

import jax
import jax.numpy as jnp
from jax import lax
from jax.experimental import pallas as pl
from jax.experimental.pallas import tpu as pltpu
from jax.sharding import PartitionSpec as P

LANES = 128
SUB = 8
PLANE = 8
SCALE = 2.0**40
VMEM = pl.BlockSpec(memory_space=pltpu.VMEM)
HBM = pl.BlockSpec(memory_space=pltpu.HBM)
PARAMS = pltpu.CompilerParams(vmem_limit_bytes=32 * 1024 * 1024)


def f32(*shape):
    return jax.ShapeDtypeStruct(shape, jnp.float32)


def tile(t):
    return pl.ds(t * LANES, LANES)


def rows_of(b):
    return pl.ds(pl.multiple_of(b * SUB, SUB), SUB)


def column(row):
    return jnp.broadcast_to(row, (LANES, LANES)).T


def fold(parts):
    sub = lax.broadcasted_iota(jnp.int32, (SUB, LANES), 0)
    order, step = list(parts), 1
    while step < SUB:
        mask = (sub & step) == 0
        merged = []
        for a, b in zip(order[0::2], order[1::2]):
            merged.append(jnp.where(mask, a, b) + pltpu.roll(jnp.where(mask, b, a), SUB - step, 0))
        order, step = merged, 2 * step
    return order[0]


def table_rows(counties):
    return 2 * counties + SUB


def seg_count(seg_ref):
    last = seg_ref.shape[0] - SUB
    return seg_ref[last : last + 1, :][0, 0]


def seg_range(seg_ref, k):
    row = seg_ref[pl.ds(k, 1), :]
    return row[0, 0], row[0, 1]


def seg_name(seg_ref, k):
    return seg_ref[pl.ds((seg_ref.shape[0] - SUB) // 2 + k, 1), :]


def message(msg_ref, row_sum, share):
    sub = lax.broadcasted_iota(jnp.int32, (SUB, LANES), 0)
    msg_ref[...] = jnp.where(sub == 0, row_sum, jnp.where(sub == 1, share, 0.0))


def first_kernel(
    chunks, cid_hbm, cid_row_hbm, goal_row_hbm, w_hbm, tgt_hbm, msg_ref, seg_ref, cols_ref, w_ref, tgt_ref, cid_ref, cid_row, goal_row, acc_w, acc_t, sems
):
    rows = w_ref.shape[1]
    counties, width = tgt_ref.shape
    tiles = width // LANES
    block = width // chunks
    wide = chunks // 2
    small = [
        pltpu.make_async_copy(cid_hbm, cid_ref, sems.at[0]),
        pltpu.make_async_copy(cid_row_hbm, cid_row, sems.at[1]),
        pltpu.make_async_copy(goal_row_hbm, goal_row, sems.at[2]),
    ]
    slabs = []
    for q in range(chunks):
        place = w_ref.at[q // wide, :, pl.ds(q % wide * block, block)]
        slabs.append(pltpu.make_async_copy(w_hbm.at[:, pl.ds(q * block, block)], place, sems.at[3 + q]))
    for copy in small + slabs:
        copy.start()
    acc_w[...] = jnp.zeros_like(acc_w)
    acc_t[...] = jnp.zeros_like(acc_t)
    for copy in small:
        copy.wait()

    low = cid_ref[0] >> 3
    high = (cid_ref[rows - 1] >> 3) + 1

    def targets(b):
        return pltpu.make_async_copy(tgt_hbm.at[rows_of(b)], tgt_ref.at[rows_of(b)], sems.at[3 + chunks + b])

    @pl.loop(low, high)
    def _(b):
        targets(b).start()

    lane = lax.broadcasted_iota(jnp.int32, (1, LANES), 1)
    n = 0
    first = 0
    for g in range(rows):
        c = cid_ref[g]
        seg_ref[pl.ds(n, 1), :] = jnp.where(lane == 0, first, (g + SUB) // SUB)
        seg_ref[pl.ds(counties + n, 1), :] = jnp.full((1, LANES), c)
        if g + 1 < rows:
            new = cid_ref[g + 1] != c
            n = n + new.astype(jnp.int32)
            first = jnp.where(new, (g + 1) // SUB, first)
    seg_ref[2 * counties : 2 * counties + SUB, :] = jnp.full((SUB, LANES), n + 1)
    cols_ref[0] = column(cid_row[...].astype(jnp.float32))
    cols_ref[1] = column(goal_row[...].astype(jnp.float32))

    for q in range(chunks):
        slabs[q].wait()

        @pl.loop(0, rows // SUB)
        def _(b):
            part = rows_of(b)
            accs = [acc_w[part, :]] + [jnp.zeros((SUB, LANES), jnp.float32)] * 3
            for i in range(block // LANES):
                accs[i % 4] = accs[i % 4] + w_ref[q // wide, part, tile(q % wide * (block // LANES) + i)]
            acc_w[part, :] = (accs[0] + accs[1]) + (accs[2] + accs[3])

    @pl.loop(low, high)
    def _(b):
        targets(b).wait()
        part = rows_of(b)
        accs = [jnp.zeros((SUB, LANES), jnp.float32)] * 4
        for t in range(tiles):
            accs[t % 4] = accs[t % 4] + tgt_ref[part, tile(t)].astype(jnp.float32)
        acc_t[part, :] = (accs[0] + accs[1]) + (accs[2] + accs[3])

    row_sum = jnp.sum(acc_w[...].T, axis=0, keepdims=True)
    share = jnp.sum(acc_t[...].T, axis=0, keepdims=True)
    message(msg_ref, row_sum, share)


def share_kernel(seg_ref, tgt_ref, share_ref):
    tiles = tgt_ref.shape[1] // LANES
    half = tiles // 2
    sub = lax.broadcasted_iota(jnp.int32, (SUB, LANES), 0)
    none = jnp.zeros((SUB, LANES), jnp.float32)

    @pl.loop(0, seg_count(seg_ref))
    def _(k):
        c = seg_name(seg_ref, k)[0, 0]
        part = rows_of(c >> 3)
        mask = sub == (c & 7)
        for h in range(2):
            own = [jnp.where(mask, tgt_ref[part, tile(h * half + t)].astype(jnp.float32), 0.0) for t in range(half)]
            own += [none] * (-half % SUB)
            for t in range(0, len(own), SUB):
                share_ref[k, h, t : t + SUB, :] = fold(own[t : t + SUB])


def side_of(mine):
    core = lax.axis_index("bg") % 2
    return core if mine else 1 - core


def sums_body(second, mine, seg_ref, w_ref, cols_ref, r1_ref, r2_ref, edge_ref, sums_ref):
    w_ref = w_ref.at[side_of(mine)]
    half = w_ref.shape[1] // LANES
    n = seg_count(seg_ref)
    sub = lax.broadcasted_iota(jnp.int32, (SUB, LANES), 0)
    none = jnp.zeros((SUB, LANES), jnp.float32)

    @pl.loop(0, n)
    def _(k):
        b0, b1 = seg_range(seg_ref, k)
        name = seg_name(seg_ref, k).astype(jnp.float32)

        def block(b, accs):
            rows = rows_of(b)
            mask = cols_ref[0, rows, :] == name
            r1 = jnp.where(mask, r1_ref[rows, :], 0.0)
            out = []
            if second:
                r2 = r2_ref[rows, :]
                for t in range(half):
                    out.append(accs[t] + w_ref[rows, tile(t)] * r1 * r2)
            else:
                for t in range(half):
                    out.append(accs[t] + w_ref[rows, tile(t)] * r1)
                out.append(accs[half] + jnp.where(mask, cols_ref[1, rows, :], 0.0))
            return tuple(out)

        parts = list(lax.fori_loop(b0, b1, block, (none,) * (half if second else half + 1)))
        if second:
            parts.append(none)
        parts.append(jnp.where(sub == 0, name, 0.0))
        parts += [none] * (-len(parts) % SUB)
        for t in range(0, len(parts), SUB):
            sums_ref[k, t : t + SUB, :] = fold(parts[t : t + SUB])

    edge_ref[0] = sums_ref[0]
    edge_ref[1] = sums_ref[n - 1]


def give_kernel(second, parts_n, *refs):
    seg_ref, refs = refs[0], refs[1:]
    msgs, refs = refs[:parts_n], refs[parts_n:]
    if second:
        w_ref, cols_ref, r1_ref, edge_ref, sums_ref, rcol_ref = refs
    else:
        _, w_ref, cols_ref, edge_ref, sums_ref, rcol_ref, total_ref = refs
        r1_ref = rcol_ref
    total = msgs[0][...]
    for m in msgs[1:]:
        total = total + m[...]
    if not second:
        total_ref[...] = total
    rcol = cols_ref[1] / column(total[0:1])
    rcol_ref[...] = rcol * SCALE if second else rcol
    sums_body(second, False, seg_ref, w_ref, cols_ref, r1_ref, rcol_ref, edge_ref, sums_ref)


def keep_kernel(second, seg_ref, w_ref, cols_ref, r1_ref, *refs):
    r2_ref = refs[0] if second else None
    edge_ref, sums_ref = refs[-2:]
    sums_body(second, True, seg_ref, w_ref, cols_ref, r1_ref, r2_ref, edge_ref, sums_ref)


def join(refs):
    rows = refs[0].shape[1]
    name = rows - 3
    sub = lax.broadcasted_iota(jnp.int32, (rows, LANES), 0)
    out = []
    for e, pick in ((0, jnp.minimum), (1, jnp.maximum)):
        names = [ref[e, name : name + 1, :] for ref in refs]
        edge = functools.reduce(pick, names)
        total = jnp.zeros((rows, LANES), jnp.float32)
        for ref, own in zip(refs, names):
            total = total + jnp.where(own == edge, ref[e], 0.0)
        out.append(jnp.where(sub == name, edge, total))
    return out


def chip_kernel(keep_ref, got_ref, chip_ref):
    head, tail = join([keep_ref, got_ref])
    chip_ref[0] = head
    chip_ref[1] = tail


def plane_kernel(*refs):
    send_ref = refs[-1]
    z = lax.axis_index("bg") // PLANE
    head, tail = join(refs[:-1])
    for j in range(send_ref.shape[0]):

        @pl.when(j > z)
        def _():
            send_ref[j] = tail

        @pl.when(j <= z)
        def _():
            send_ref[j] = head


def edge_kernel(keep_ref, got_ref, far_ref, *refs):
    chips, (own_ref, other_ref) = refs[:-2], refs[-2:]
    planes, rows = far_ref.shape[:2]
    me = lax.axis_index("bg")
    z = me // PLANE
    x = (me // 2) % (PLANE // 2)
    core = me % 2
    name = rows - 3
    sub = lax.broadcasted_iota(jnp.int32, (rows, LANES), 0)

    for mine_ref, near_ref, out_ref, side in ((keep_ref, got_ref, own_ref, core), (got_ref, keep_ref, other_ref, 1 - core)):
        for e in range(2):
            county = mine_ref[e, name : name + 1, :]
            total = mine_ref[e]

            def add(total, ref, county=county):
                return total + jnp.where(ref[name : name + 1, :] == county, ref[...], 0.0)

            total = add(total, near_ref.at[side])
            for m, chip_ref in enumerate(chips, 1):
                total = add(total, chip_ref.at[jnp.where((x ^ m) < x, 1, 0)])
            for j in range(planes):
                hit = jnp.logical_and(far_ref[j, name : name + 1, :] == county, j != z)
                total = total + jnp.where(hit, far_ref[j], 0.0)
            out_ref[e] = total


def each_sum(n, edge_ref, sums_ref, body):
    body(0, edge_ref.at[0])
    body(n - 1, edge_ref.at[1])

    @pl.loop(1, n - 1)
    def _(k):
        body(k, sums_ref.at[k])


def rows_kernel(mine, seg_ref, total_ref, w_ref, cols_ref, r1_ref, sums_ref, edge_ref, share_ref, *refs):
    if mine:
        goal_ref, acc_ref, fac_ref = refs
    else:
        part_ref, goal_ref, msg_ref, fac_ref, acc_ref = refs
    w_ref = w_ref.at[side_of(mine)]
    half = w_ref.shape[1] // LANES
    side = side_of(mine)
    n = seg_count(seg_ref)
    share = total_ref[1:2, :]
    lane = lax.broadcasted_iota(jnp.int32, (1, LANES), 1)

    def factor(k, sum_ref):
        whole = jnp.sum(jnp.where(lane == seg_name(seg_ref, k), share, 0.0), axis=1, keepdims=True)
        goal = share_ref[k, side] * (sum_ref[half : half + 1, :] / whole)
        goal_ref[k] = goal
        fac_ref[k] = goal / sum_ref[...]

    each_sum(n, edge_ref, sums_ref, factor)
    acc_ref[...] = jnp.zeros_like(acc_ref) if mine else part_ref[...]

    @pl.loop(0, n)
    def _(k):
        b0, b1 = seg_range(seg_ref, k)
        name = seg_name(seg_ref, k).astype(jnp.float32)

        @pl.loop(b0, b1)
        def _(b):
            rows = rows_of(b)
            mask = cols_ref[0, rows, :] == name
            r1 = jnp.where(mask, r1_ref[rows, :], 0.0)
            sums = [None] * 4
            for t in range(half):
                x = w_ref[rows, tile(t)] * r1 * fac_ref[k, t : t + 1, :]
                sums[t % 4] = x if sums[t % 4] is None else sums[t % 4] + x
            acc_ref[rows, :] += (sums[0] + sums[1]) + (sums[2] + sums[3])

    if not mine:
        message(msg_ref, jnp.sum(acc_ref[...].T, axis=0, keepdims=True), jnp.zeros((1, LANES), jnp.float32))


def fitted(mine, chunks, done, seg_ref, w_ref, cols_ref, r1_ref, r2_ref, goal_ref, sums_ref, edge_ref, out_ref, fac_ref):
    w_ref = w_ref.at[side_of(mine)]
    half = w_ref.shape[1] // LANES
    n = seg_count(seg_ref)

    def factor(k, sum_ref):
        fac_ref[k] = 100.0 * (goal_ref[k] / sum_ref[...])

    each_sum(n, edge_ref, sums_ref, factor)
    for q in range(chunks):
        own = range(q * half // chunks, (q + 1) * half // chunks)

        @pl.loop(0, n)
        def _(k):
            b0, b1 = seg_range(seg_ref, k)
            name = seg_name(seg_ref, k).astype(jnp.float32)
            fac = [jnp.broadcast_to(fac_ref[k, t : t + 1, :], (SUB, LANES)) for t in own]

            @pl.loop(b0, b1)
            def _(b):
                rows = rows_of(b)
                mask = cols_ref[0, rows, :] == name
                r1 = r1_ref[rows, :]
                r2 = r2_ref[rows, :]
                for i, t in enumerate(own):
                    x = w_ref[rows, tile(t)] * r1 * r2 * fac[i]
                    pltpu.store(out_ref.at[rows, tile(t)], x, mask=mask)

        done(q)


def last_own_kernel(seg_ref, w_ref, cols_ref, r1_ref, r2_ref, goal_ref, sums_ref, edge_ref, out_ref, fac_ref):
    fitted(True, 1, lambda q: None, seg_ref, w_ref, cols_ref, r1_ref, r2_ref, goal_ref, sums_ref, edge_ref, out_ref, fac_ref)


def last_kernel(
    chunks, seg_ref, w_ref, cols_ref, r1_ref, r2_ref, goal_ref, sums_ref, edge_ref, own_ref, out_hbm, out_ref, fac_ref, sems
):
    width = w_ref.shape[2]
    block = width // chunks

    def place(mine, at, size):
        start = side_of(mine) * width + at
        return out_hbm.at[:, pl.ds(pl.multiple_of(start, LANES), size)]

    copies = []
    for q in range(chunks):
        part = pl.ds(q * block, block)
        copies.append(pltpu.make_async_copy(own_ref.at[:, part], place(True, q * block, block), sems.at[chunks + q]))
        copies[q].start()

    def done(q):
        copy = pltpu.make_async_copy(out_ref.at[:, pl.ds(q * block, block)], place(False, q * block, block), sems.at[q])
        copy.start()
        copies.append(copy)

    fitted(False, chunks, done, seg_ref, w_ref, cols_ref, r1_ref, r2_ref, goal_ref, sums_ref, edge_ref, out_ref, fac_ref)
    for copy in copies:
        copy.wait()


def call(kernel, name, ins, in_specs, out_shape, out_specs=None, scratch=()):
    if out_specs is None:
        out_specs = jax.tree.map(lambda _: VMEM, out_shape)
    return pl.pallas_call(
        kernel,
        out_shape=out_shape,
        in_specs=in_specs,
        out_specs=out_specs,
        scratch_shapes=scratch,
        compiler_params=PARAMS,
        cost_estimate=pl.CostEstimate(flops=4 << 20, bytes_accessed=4 << 20, transcendentals=0),
        name=name,
    )(*ins)


def local(planes, parts, seed_slab, row_target, county_id, county_target):
    rows, width = seed_slab.shape
    counties = county_target.shape[0]
    half = width // LANES // 2
    half_rows = half + 4
    in_chunks, out_chunks = 8, 2
    device = planes * PLANE

    edge = f32(2, half_rows, LANES)
    table = f32(counties, half_rows, LANES)
    column_of = f32(rows, LANES)
    small = f32(SUB, LANES)
    msg, seg, cols, slab, targets = call(
        functools.partial(first_kernel, in_chunks),
        "row_sums_1",
        [
            pltpu.with_memory_space_constraint(x, pltpu.HBM)
            for x in (county_id, county_id.reshape(1, rows), row_target.reshape(1, rows), seed_slab, county_target)
        ],
        [HBM] * 5,
        (small, jax.ShapeDtypeStruct((table_rows(counties), LANES), jnp.int32), f32(2, rows, LANES), f32(2, rows, width // 2), jax.ShapeDtypeStruct((counties, width), jnp.int32)),
        (VMEM, VMEM, VMEM, VMEM, VMEM),
        [
            pltpu.SMEM((rows,), jnp.int32),
            pltpu.VMEM((1, rows), jnp.int32),
            pltpu.VMEM((1, rows), jnp.int32),
            pltpu.VMEM((rows, LANES), jnp.float32),
            pltpu.VMEM((LANES, LANES), jnp.float32),
            pltpu.SemaphoreType.DMA((3 + in_chunks + counties // SUB,)),
        ],
    )

    def swap(x, axis, size, mask):
        return lax.ppermute(x, axis, [(i, i ^ mask) for i in range(size)])

    def over_type(x):
        return [x] + [swap(x, "type", parts, m) for m in range(1, parts)]

    lines = [[PLANE * z + s for z in range(planes)] for s in range(PLANE)]

    def edges(give, keep):
        got = swap(give, "bg", device, 1)
        keep = keep()
        chip = call(chip_kernel, "chip_sums", (keep[0], got), [VMEM] * 2, edge)
        chips = [swap(chip, "bg", device, 2 * m) for m in range(1, PLANE // 2)]
        send = call(plane_kernel, "plane_sums", [chip] + chips, [VMEM] * (PLANE // 2), f32(planes, half_rows, LANES))
        far = lax.all_to_all(send, "bg", 0, 0, axis_index_groups=lines)
        own, other = call(edge_kernel, "edge_sums", [keep[0], got, far] + chips, [VMEM] * (2 + PLANE // 2), (edge, edge))
        return own, swap(other, "bg", device, 1), keep[1]

    msgs = over_type(msg)
    share = call(share_kernel, "shares", (seg, targets), [VMEM, VMEM], f32(counties, 2, half_rows, LANES))
    give, sums_give, r1, total = call(
        functools.partial(give_kernel, False, parts),
        "county_sums_1a",
        [seg] + msgs + [share, slab, cols],
        [VMEM] * (parts + 4),
        (edge, table, column_of, small),
    )
    own, other, sums_keep = edges(
        give,
        lambda: call(functools.partial(keep_kernel, False), "county_sums_1b", (seg, slab, cols, r1), [VMEM] * 4, (edge, table)),
    )
    fac = pltpu.VMEM((counties, half_rows, LANES), jnp.float32)
    goal_keep, part = call(
        functools.partial(rows_kernel, True),
        "row_sums_2a",
        (seg, total, slab, cols, r1, sums_keep, own, share),
        [VMEM] * 8,
        (table, column_of),
        None,
        [fac],
    )
    goal_give, msg = call(
        functools.partial(rows_kernel, False),
        "row_sums_2b",
        (seg, total, slab, cols, r1, sums_give, other, share, part),
        [VMEM] * 9,
        (table, small),
        None,
        [fac, pltpu.VMEM((rows, LANES), jnp.float32)],
    )
    give, sums_give, r2 = call(
        functools.partial(give_kernel, True, parts),
        "county_sums_2a",
        [seg] + over_type(msg) + [slab, cols, r1],
        [VMEM] * (parts + 4),
        (edge, table, column_of),
    )
    own, other, sums_keep = edges(
        give,
        lambda: call(functools.partial(keep_kernel, True), "county_sums_2b", (seg, slab, cols, r1, r2), [VMEM] * 5, (edge, table)),
    )
    mine = call(
        last_own_kernel,
        "fitted_a",
        (seg, slab, cols, r1, r2, goal_keep, sums_keep, own),
        [VMEM] * 8,
        f32(rows, width // 2),
        None,
        [fac],
    )
    return call(
        functools.partial(last_kernel, out_chunks),
        "fitted_b",
        (seg, slab, cols, r1, r2, goal_give, sums_give, other, mine),
        [VMEM] * 9,
        f32(rows, width),
        HBM,
        [pltpu.VMEM((rows, width // 2), jnp.float32), fac, pltpu.SemaphoreType.DMA((2 * out_chunks,))],
    )


def solution(mesh):
    return jax.shard_map(
        functools.partial(local, mesh.shape["bg"] // PLANE, mesh.shape["type"]),
        mesh=mesh,
        in_specs=(P("bg", "type"), P("bg"), P("bg"), P(None, "type")),
        out_specs=P("bg", "type"),
        check_vma=False,
    )
```

```python
import functools

import jax
import jax.numpy as jnp
from jax import lax
from jax.experimental import pallas as pl
from jax.experimental.pallas import tpu as pltpu
from jax.sharding import PartitionSpec as P

LANES = 128
SUB = 8
CHUNKS = 4
PLANE = 8
SCALE = 2.0**40
VMEM = pl.BlockSpec(memory_space=pltpu.VMEM)
HBM = pl.BlockSpec(memory_space=pltpu.HBM)
PARAMS = pltpu.CompilerParams(vmem_limit_bytes=32 * 1024 * 1024)


def f32(*shape):
    return jax.ShapeDtypeStruct(shape, jnp.float32)


def tile(t):
    return pl.ds(t * LANES, LANES)


def rows_of(b):
    return pl.ds(pl.multiple_of(b * SUB, SUB), SUB)


def column(row):
    return jnp.broadcast_to(row, (LANES, LANES)).T


def fold(parts):
    sub = lax.broadcasted_iota(jnp.int32, (SUB, LANES), 0)
    order, step = list(parts), 1
    while step < SUB:
        mask = (sub & step) == 0
        merged = []
        for a, b in zip(order[0::2], order[1::2]):
            merged.append(jnp.where(mask, a, b) + pltpu.roll(jnp.where(mask, b, a), SUB - step, 0))
        order, step = merged, 2 * step
    return order[0]


PAIRS = 80


def table_rows(counties):
    return 2 * counties + PAIRS + SUB


def seg_number(seg_ref, row):
    return seg_ref[pl.ds(row, 1), :][0, 0]


def seg_counties(seg_ref):
    return (seg_ref.shape[0] - SUB - PAIRS) // 2


def seg_counts(seg_ref):
    both = seg_number(seg_ref, seg_ref.shape[0] - SUB)
    return both & 255, both >> 8


def seg_name(seg_ref, k):
    return seg_ref[pl.ds(seg_counties(seg_ref) + k, 1), :]


def each_pair(seg_ref, cols_ref, body):
    at = 2 * seg_counties(seg_ref)

    def step(p, pair):
        following = seg_number(seg_ref, at + p + 1)
        k = pair >> 8
        rows = rows_of(pair & 255)
        mask = cols_ref[0, rows, :] == seg_name(seg_ref, k).astype(jnp.float32)
        body(k, rows, mask)
        return following

    lax.fori_loop(0, seg_counts(seg_ref)[1], step, seg_number(seg_ref, at))


def message(msg_ref, row_sum, share):
    sub = lax.broadcasted_iota(jnp.int32, (SUB, LANES), 0)
    msg_ref[...] = jnp.where(sub == 0, row_sum, jnp.where(sub == 1, share, 0.0))


def first_kernel(cid_hbm, w_hbm, tgt_hbm, msg_ref, w_ref, tgt_ref, cid_ref, acc_w, acc_t, sems):
    rows = w_ref.shape[1]
    counties, width = tgt_ref.shape
    tiles = width // LANES
    chunks = CHUNKS
    block = width // chunks
    wide = chunks // 2
    county_ids = pltpu.make_async_copy(cid_hbm, cid_ref, sems.at[0])
    county_ids.start()
    slabs = []
    for q in range(chunks):
        place = w_ref.at[q // wide, :, pl.ds(q % wide * block, block)]
        slabs.append(pltpu.make_async_copy(w_hbm.at[:, pl.ds(q * block, block)], place, sems.at[1 + q]))
        slabs[q].start()
    acc_w[...] = jnp.zeros_like(acc_w)
    acc_t[...] = jnp.zeros_like(acc_t)
    county_ids.wait()

    low = cid_ref[0] >> 3
    high = (cid_ref[rows - 1] >> 3) + 1

    def targets(b):
        return pltpu.make_async_copy(tgt_hbm.at[rows_of(b)], tgt_ref.at[rows_of(b)], sems.at[1 + chunks + b])

    @pl.loop(low, high)
    def _(b):
        targets(b).start()

    for q in range(chunks):
        slabs[q].wait()

        @pl.loop(0, rows // SUB)
        def _(b):
            part = rows_of(b)
            accs = [acc_w[part, :]] + [jnp.zeros((SUB, LANES), jnp.float32)] * 3
            for i in range(block // LANES):
                accs[i % 4] = accs[i % 4] + w_ref[q // wide, part, tile(q % wide * (block // LANES) + i)]
            acc_w[part, :] = (accs[0] + accs[1]) + (accs[2] + accs[3])

    @pl.loop(low, high)
    def _(b):
        targets(b).wait()
        part = rows_of(b)
        accs = [jnp.zeros((SUB, LANES), jnp.float32)] * 4
        for t in range(tiles):
            accs[t % 4] = accs[t % 4] + tgt_ref[part, tile(t)].astype(jnp.float32)
        acc_t[part, :] = (accs[0] + accs[1]) + (accs[2] + accs[3])

    row_sum = jnp.sum(acc_w[...].T, axis=0, keepdims=True)
    share = jnp.sum(acc_t[...].T, axis=0, keepdims=True)
    message(msg_ref, row_sum, share)


def prepare_kernel(cid_hbm, cid_row_hbm, goal_row_hbm, tgt_ref, seg_ref, cols_ref, share_ref, cid_ref, cid_row, goal_row, sems):
    copies = [
        pltpu.make_async_copy(cid_hbm, cid_ref, sems.at[0]),
        pltpu.make_async_copy(cid_row_hbm, cid_row, sems.at[1]),
        pltpu.make_async_copy(goal_row_hbm, goal_row, sems.at[2]),
    ]
    for copy in copies:
        copy.start()
    for copy in copies:
        copy.wait()
    rows = cid_ref.shape[0]
    counties, width = tgt_ref.shape
    half = width // LANES // 2
    n, p, first = 0, 0, 0
    for g in range(rows):
        c = cid_ref[g]
        b = g // SUB
        if g and g % SUB == 0:
            p = p + 1
        seg_ref[pl.ds(n, 1), :] = jnp.full((1, LANES), first + 256 * (b + 1))
        seg_ref[pl.ds(counties + n, 1), :] = jnp.full((1, LANES), c)
        seg_ref[pl.ds(2 * counties + p, 1), :] = jnp.full((1, LANES), b + 256 * n)
        if g + 1 < rows:
            new = cid_ref[g + 1] != c
            step = new.astype(jnp.int32)
            n = n + step
            first = jnp.where(new, (g + 1) // SUB, first)
            if (g + 1) % SUB:
                p = p + step
    last = 2 * counties + PAIRS
    seg_ref[last : last + SUB, :] = jnp.full((SUB, LANES), n + 1 + 256 * (p + 1))
    cols_ref[0] = column(cid_row[...].astype(jnp.float32))
    cols_ref[1] = column(goal_row[...].astype(jnp.float32))

    sub = lax.broadcasted_iota(jnp.int32, (SUB, LANES), 0)
    none = jnp.zeros((SUB, LANES), jnp.float32)

    @pl.loop(0, n + 1)
    def _(k):
        c = seg_name(seg_ref, k)[0, 0]
        part = rows_of(c >> 3)
        mask = sub == (c & 7)
        for h in range(2):
            own = [jnp.where(mask, tgt_ref[part, tile(h * half + t)].astype(jnp.float32), 0.0) for t in range(half)]
            own += [none] * (-half % SUB)
            for t in range(0, len(own), SUB):
                share_ref[k, h, t : t + SUB, :] = fold(own[t : t + SUB])


def side_of(mine):
    core = lax.axis_index("bg") % 2
    return core if mine else 1 - core


def sums_body(second, mine, seg_ref, w_ref, cols_ref, r1_ref, r2_ref, edge_ref, sums_ref, parts_ref):
    w_ref = w_ref.at[side_of(mine)]
    half = w_ref.shape[1] // LANES
    n = seg_counts(seg_ref)[0]
    sub = lax.broadcasted_iota(jnp.int32, (SUB, LANES), 0)
    none = jnp.zeros((SUB, LANES), jnp.float32)

    def county(k, place):
        name = seg_name(seg_ref, k).astype(jnp.float32)

        def block(b, accs):
            rows = rows_of(b)
            mask = cols_ref[0, rows, :] == name
            r1 = jnp.where(mask, r1_ref[rows, :], 0.0)
            out = []
            if second:
                r2 = r2_ref[rows, :]
                for t in range(half):
                    out.append(accs[t] + w_ref[rows, tile(t)] * r1 * r2)
            else:
                for t in range(half):
                    out.append(accs[t] + w_ref[rows, tile(t)] * r1)
                out.append(accs[half] + jnp.where(mask, cols_ref[1, rows, :], 0.0))
            return tuple(out)

        parts = list(lax.fori_loop(place & 255, place >> 8, block, (none,) * (half if second else half + 1)))
        following = seg_number(seg_ref, k + 1)
        if second:
            parts.append(none)
        parts.append(jnp.where(sub == 0, name, 0.0))
        parts += [none] * (-len(parts) % SUB)
        for i, part in enumerate(parts):
            parts_ref[i * SUB : (i + 1) * SUB, :] = part
        for t in range(0, len(parts), SUB):
            folded = [parts_ref[pl.ds(t * SUB + i, SUB, stride=SUB), :] for i in range(SUB)]
            while len(folded) > 1:
                folded = [x + y for x, y in zip(folded[0::2], folded[1::2])]
            sums_ref[k, t : t + SUB, :] = folded[0]
        return following

    lax.fori_loop(0, n, county, seg_number(seg_ref, 0))
    edge_ref[0] = sums_ref[0]
    edge_ref[1] = sums_ref[n - 1]


def give_kernel(second, parts_n, *refs):
    seg_ref, refs = refs[0], refs[1:]
    msgs, refs, parts_ref = refs[:parts_n], refs[parts_n:-1], refs[-1]
    if second:
        w_ref, cols_ref, r1_ref, edge_ref, sums_ref, rcol_ref = refs
    else:
        _, w_ref, cols_ref, edge_ref, sums_ref, rcol_ref, total_ref = refs
        r1_ref = rcol_ref
    total = msgs[0][...]
    for m in msgs[1:]:
        total = total + m[...]
    if not second:
        total_ref[...] = total
    rcol = cols_ref[1] / column(total[0:1])
    rcol_ref[...] = rcol * SCALE if second else rcol
    sums_body(second, False, seg_ref, w_ref, cols_ref, r1_ref, rcol_ref, edge_ref, sums_ref, parts_ref)


def keep_kernel(second, seg_ref, w_ref, cols_ref, r1_ref, *refs):
    r2_ref = refs[0] if second else None
    sums_body(second, True, seg_ref, w_ref, cols_ref, r1_ref, r2_ref, *refs[-3:])


def join(refs):
    rows = refs[0].shape[1]
    name = rows - 3
    sub = lax.broadcasted_iota(jnp.int32, (rows, LANES), 0)
    out = []
    for e, pick in ((0, jnp.minimum), (1, jnp.maximum)):
        names = [ref[e, name : name + 1, :] for ref in refs]
        edge = functools.reduce(pick, names)
        total = jnp.zeros((rows, LANES), jnp.float32)
        for ref, own in zip(refs, names):
            total = total + jnp.where(own == edge, ref[e], 0.0)
        out.append(jnp.where(sub == name, edge, total))
    return out


def chip_kernel(keep_ref, got_ref, chip_ref):
    head, tail = join([keep_ref, got_ref])
    chip_ref[0] = head
    chip_ref[1] = tail


def plane_kernel(*refs):
    send_ref = refs[-1]
    z = lax.axis_index("bg") // PLANE
    head, tail = join(refs[:-1])
    for j in range(send_ref.shape[0]):

        @pl.when(j > z)
        def _():
            send_ref[j] = tail

        @pl.when(j <= z)
        def _():
            send_ref[j] = head


def edge_kernel(keep_ref, got_ref, far_ref, *refs):
    chips, (own_ref, other_ref) = refs[:-2], refs[-2:]
    planes, rows = far_ref.shape[:2]
    me = lax.axis_index("bg")
    z = me // PLANE
    x = (me // 2) % (PLANE // 2)
    core = me % 2
    name = rows - 3
    sub = lax.broadcasted_iota(jnp.int32, (rows, LANES), 0)

    for mine_ref, near_ref, out_ref, side in ((keep_ref, got_ref, own_ref, core), (got_ref, keep_ref, other_ref, 1 - core)):
        for e in range(2):
            county = mine_ref[e, name : name + 1, :]
            total = mine_ref[e]

            def add(total, ref, county=county):
                return total + jnp.where(ref[name : name + 1, :] == county, ref[...], 0.0)

            total = add(total, near_ref.at[side])
            for m, chip_ref in enumerate(chips, 1):
                total = add(total, chip_ref.at[jnp.where((x ^ m) < x, 1, 0)])
            for j in range(planes):
                hit = jnp.logical_and(far_ref[j, name : name + 1, :] == county, j != z)
                total = total + jnp.where(hit, far_ref[j], 0.0)
            out_ref[e] = total


def each_sum(n, edge_ref, sums_ref, body):
    group = 4

    @pl.when(n > 2)
    def _():
        @pl.loop(0, (n + group - 1) // group)
        def _(g):
            for i in range(group):
                body(g * group + i, sums_ref.at[g * group + i])

    body(0, edge_ref.at[0])
    body(n - 1, edge_ref.at[1])


def rows_kernel(mine, seg_ref, total_ref, w_ref, cols_ref, r1_ref, sums_ref, edge_ref, share_ref, *refs):
    if mine:
        goal_ref, acc_ref, fac_ref = refs
    else:
        part_ref, goal_ref, msg_ref, fac_ref, acc_ref = refs
    w_ref = w_ref.at[side_of(mine)]
    half = w_ref.shape[1] // LANES
    side = side_of(mine)
    n = seg_counts(seg_ref)[0]
    share = total_ref[1:2, :]
    lane = lax.broadcasted_iota(jnp.int32, (1, LANES), 1)

    def factor(k, sum_ref):
        whole = jnp.sum(jnp.where(lane == seg_name(seg_ref, k), share, 0.0), axis=1, keepdims=True)
        goal = share_ref[k, side] * (sum_ref[half : half + 1, :] / whole)
        goal_ref[k] = goal
        fac_ref[k] = goal / sum_ref[...]

    each_sum(n, edge_ref, sums_ref, factor)
    acc_ref[...] = jnp.zeros_like(acc_ref) if mine else part_ref[...]

    def pair(k, rows, mask):
        r1 = jnp.where(mask, r1_ref[rows, :], 0.0)
        sums = [None] * 4
        for t in range(half):
            x = w_ref[rows, tile(t)] * r1 * fac_ref[k, t : t + 1, :]
            sums[t % 4] = x if sums[t % 4] is None else sums[t % 4] + x
        acc_ref[rows, :] += (sums[0] + sums[1]) + (sums[2] + sums[3])

    each_pair(seg_ref, cols_ref, pair)
    if not mine:
        message(msg_ref, jnp.sum(acc_ref[...].T, axis=0, keepdims=True), jnp.zeros((1, LANES), jnp.float32))


def fitted(mine, chunks, done, seg_ref, w_ref, cols_ref, r1_ref, r2_ref, goal_ref, sums_ref, edge_ref, out_ref, fac_ref):
    w_ref = w_ref.at[side_of(mine)]
    half = w_ref.shape[1] // LANES
    n = seg_counts(seg_ref)[0]

    def factor(k, sum_ref):
        fac_ref[k] = 100.0 * (goal_ref[k] / sum_ref[...])

    each_sum(n, edge_ref, sums_ref, factor)
    for q in range(chunks):
        own = range(q * half // chunks, (q + 1) * half // chunks)

        def pair(k, rows, mask):
            r1 = r1_ref[rows, :]
            r2 = r2_ref[rows, :]
            for t in own:
                x = w_ref[rows, tile(t)] * r1 * r2 * fac_ref[k, t : t + 1, :]
                pltpu.store(out_ref.at[rows, tile(t)], x, mask=mask)

        each_pair(seg_ref, cols_ref, pair)
        done(q)


def last_own_kernel(seg_ref, w_ref, cols_ref, r1_ref, r2_ref, goal_ref, sums_ref, edge_ref, out_ref, fac_ref):
    fitted(True, 1, lambda q: None, seg_ref, w_ref, cols_ref, r1_ref, r2_ref, goal_ref, sums_ref, edge_ref, out_ref, fac_ref)


def last_kernel(
    chunks, seg_ref, w_ref, cols_ref, r1_ref, r2_ref, goal_ref, sums_ref, edge_ref, own_ref, out_hbm, out_ref, fac_ref, sems
):
    width = w_ref.shape[2]
    block = width // chunks

    def place(mine, at, size):
        start = side_of(mine) * width + at
        return out_hbm.at[:, pl.ds(pl.multiple_of(start, LANES), size)]

    copies = []
    for q in range(chunks):
        part = pl.ds(q * block, block)
        copies.append(pltpu.make_async_copy(own_ref.at[:, part], place(True, q * block, block), sems.at[chunks + q]))
        copies[q].start()

    def done(q):
        copy = pltpu.make_async_copy(out_ref.at[:, pl.ds(q * block, block)], place(False, q * block, block), sems.at[q])
        copy.start()
        copies.append(copy)

    fitted(False, chunks, done, seg_ref, w_ref, cols_ref, r1_ref, r2_ref, goal_ref, sums_ref, edge_ref, out_ref, fac_ref)
    for copy in copies:
        copy.wait()


def call(kernel, name, ins, in_specs, out_shape, out_specs=None, scratch=()):
    if out_specs is None:
        out_specs = jax.tree.map(lambda _: VMEM, out_shape)
    return pl.pallas_call(
        kernel,
        out_shape=out_shape,
        in_specs=in_specs,
        out_specs=out_specs,
        scratch_shapes=scratch,
        compiler_params=PARAMS,
        cost_estimate=pl.CostEstimate(flops=4 << 20, bytes_accessed=4 << 20, transcendentals=0),
        name=name,
    )(*ins)


def local(planes, parts, seed_slab, row_target, county_id, county_target):
    rows, width = seed_slab.shape
    counties = county_target.shape[0]
    half = width // LANES // 2
    half_rows = half + 4
    out_chunks = 1
    device = planes * PLANE

    edge = f32(2, half_rows, LANES)
    table = f32(counties, half_rows, LANES)
    column_of = f32(rows, LANES)
    small = f32(SUB, LANES)
    parts_scratch = [pltpu.VMEM((half_rows * SUB, LANES), jnp.float32)]
    hbm = [pltpu.with_memory_space_constraint(x, pltpu.HBM) for x in (county_id, county_id.reshape(1, rows), row_target.reshape(1, rows))]
    msg, slab, targets = call(
        first_kernel,
        "row_sums_1",
        [hbm[0]] + [pltpu.with_memory_space_constraint(x, pltpu.HBM) for x in (seed_slab, county_target)],
        [HBM] * 3,
        (small, f32(2, rows, width // 2), jax.ShapeDtypeStruct((counties, width), jnp.int32)),
        None,
        [
            pltpu.SMEM((rows,), jnp.int32),
            pltpu.VMEM((rows, LANES), jnp.float32),
            pltpu.VMEM((LANES, LANES), jnp.float32),
            pltpu.SemaphoreType.DMA((1 + CHUNKS + counties // SUB,)),
        ],
    )

    def swap(x, axis, size, mask):
        return lax.ppermute(x, axis, [(i, i ^ mask) for i in range(size)])

    def over_type(x):
        return [x] + [swap(x, "type", parts, m) for m in range(1, parts)]

    lines = [[PLANE * z + s for z in range(planes)] for s in range(PLANE)]

    def edges(give, keep):
        got = swap(give, "bg", device, 1)
        keep = keep()
        chip = call(chip_kernel, "chip_sums", (keep[0], got), [VMEM] * 2, edge)
        chips = [swap(chip, "bg", device, 2 * m) for m in range(1, PLANE // 2)]
        send = call(plane_kernel, "plane_sums", [chip] + chips, [VMEM] * (PLANE // 2), f32(planes, half_rows, LANES))
        far = lax.all_to_all(send, "bg", 0, 0, axis_index_groups=lines)
        own, other = call(edge_kernel, "edge_sums", [keep[0], got, far] + chips, [VMEM] * (2 + PLANE // 2), (edge, edge))
        return own, swap(other, "bg", device, 1), keep[1]

    msgs = over_type(msg)
    seg, cols, share = call(
        prepare_kernel,
        "prepare",
        hbm + [targets],
        [HBM] * 3 + [VMEM],
        (jax.ShapeDtypeStruct((table_rows(counties), LANES), jnp.int32), f32(2, rows, LANES), f32(counties, 2, half_rows, LANES)),
        None,
        [
            pltpu.SMEM((rows,), jnp.int32),
            pltpu.VMEM((1, rows), jnp.int32),
            pltpu.VMEM((1, rows), jnp.int32),
            pltpu.SemaphoreType.DMA((3,)),
        ],
    )
    give, sums_give, r1, total = call(
        functools.partial(give_kernel, False, parts),
        "county_sums_1a",
        [seg] + msgs + [share, slab, cols],
        [VMEM] * (parts + 4),
        (edge, table, column_of, small),
        None,
        parts_scratch,
    )
    own, other, sums_keep = edges(
        give,
        lambda: call(functools.partial(keep_kernel, False), "county_sums_1b", (seg, slab, cols, r1), [VMEM] * 4, (edge, table), None, parts_scratch),
    )
    fac = pltpu.VMEM((counties, half_rows, LANES), jnp.float32)
    goal_keep, part = call(
        functools.partial(rows_kernel, True),
        "row_sums_2a",
        (seg, total, slab, cols, r1, sums_keep, own, share),
        [VMEM] * 8,
        (table, column_of),
        None,
        [fac],
    )
    goal_give, msg = call(
        functools.partial(rows_kernel, False),
        "row_sums_2b",
        (seg, total, slab, cols, r1, sums_give, other, share, part),
        [VMEM] * 9,
        (table, small),
        None,
        [fac, pltpu.VMEM((rows, LANES), jnp.float32)],
    )
    give, sums_give, r2 = call(
        functools.partial(give_kernel, True, parts),
        "county_sums_2a",
        [seg] + over_type(msg) + [slab, cols, r1],
        [VMEM] * (parts + 4),
        (edge, table, column_of),
        None,
        parts_scratch,
    )
    own, other, sums_keep = edges(
        give,
        lambda: call(functools.partial(keep_kernel, True), "county_sums_2b", (seg, slab, cols, r1, r2), [VMEM] * 5, (edge, table), None, parts_scratch),
    )
    mine = call(
        last_own_kernel,
        "fitted_a",
        (seg, slab, cols, r1, r2, goal_keep, sums_keep, own),
        [VMEM] * 8,
        f32(rows, width // 2),
        None,
        [fac],
    )
    return call(
        functools.partial(last_kernel, out_chunks),
        "fitted_b",
        (seg, slab, cols, r1, r2, goal_give, sums_give, other, mine),
        [VMEM] * 9,
        f32(rows, width),
        HBM,
        [pltpu.VMEM((rows, width // 2), jnp.float32), fac, pltpu.SemaphoreType.DMA((2 * out_chunks,))],
    )


def solution(mesh):
    return jax.shard_map(
        functools.partial(local, mesh.shape["bg"] // PLANE, mesh.shape["type"]),
        mesh=mesh,
        in_specs=(P("bg", "type"), P("bg"), P("bg"), P(None, "type")),
        out_specs=P("bg", "type"),
        check_vma=False,
    )
```

```python
import functools

import jax
import jax.numpy as jnp
from jax import lax
from jax.experimental import pallas as pl
from jax.experimental.pallas import tpu as pltpu
from jax.sharding import PartitionSpec as P

LANES = 128
SUB = 8
PLANE = 8
SCALE = 2.0**30
SHARE = 2.0**-26
VMEM = pl.BlockSpec(memory_space=pltpu.VMEM)
HBM = pl.BlockSpec(memory_space=pltpu.HBM)
PARAMS = pltpu.CompilerParams(vmem_limit_bytes=32 * 1024 * 1024)


def f32(*shape):
    return jax.ShapeDtypeStruct(shape, jnp.float32)


def tile(t):
    return pl.ds(t * LANES, LANES)


def rows_of(b):
    return pl.ds(pl.multiple_of(b * SUB, SUB), SUB)


def column(row):
    return jnp.broadcast_to(row, (LANES, LANES)).T


def fold(parts):
    sub = lax.broadcasted_iota(jnp.int32, (SUB, LANES), 0)
    order, step = list(parts), 1
    while step < SUB:
        mask = (sub & step) == 0
        merged = []
        for a, b in zip(order[0::2], order[1::2]):
            merged.append(jnp.where(mask, a, b) + pltpu.roll(jnp.where(mask, b, a), SUB - step, 0))
        order, step = merged, 2 * step
    return order[0]


PAIRS = 80


def table_rows(counties):
    return 2 * counties + PAIRS + SUB


def seg_number(seg_ref, row):
    return seg_ref[pl.ds(row, 1), :][0, 0]


def seg_counties(seg_ref):
    return (seg_ref.shape[0] - SUB - PAIRS) // 2


def seg_counts(seg_ref):
    both = seg_number(seg_ref, seg_ref.shape[0] - SUB)
    return both & 255, both >> 8


def seg_name(seg_ref, k):
    return seg_ref[pl.ds(seg_counties(seg_ref) + k, 1), :]


def each_pair(seg_ref, cols_ref, body):
    at = 2 * seg_counties(seg_ref)

    def step(p, pair):
        following = seg_number(seg_ref, at + p + 1)
        k = pair >> 8
        rows = rows_of(pair & 255)
        mask = cols_ref[0, rows, :] == seg_name(seg_ref, k).astype(jnp.float32)
        body(k, rows, mask)
        return following

    lax.fori_loop(0, seg_counts(seg_ref)[1], step, seg_number(seg_ref, at))


def message(msg_ref, row_sum, share):
    sub = lax.broadcasted_iota(jnp.int32, (SUB, LANES), 0)
    msg_ref[...] = jnp.where(sub == 0, row_sum, jnp.where(sub == 1, share, 0.0))


def first_kernel(w_hbm, msg_ref, w_ref, acc_w, sems):
    rows, half = w_ref.shape[1:]
    tiles = half // LANES
    cuts = [[0, tiles // 2, tiles], [0, tiles // 2, 5 * tiles // 6, tiles]]
    slabs = []
    for h, cut in enumerate(cuts):
        for low, high in zip(cut, cut[1:]):
            size = (high - low) * LANES
            from_hbm = w_hbm.at[:, pl.ds(h * half + low * LANES, size)]
            copy = pltpu.make_async_copy(from_hbm, w_ref.at[h, :, pl.ds(low * LANES, size)], sems.at[len(slabs)])
            copy.start()
            slabs.append((copy, h, low, high))
    acc_w[...] = jnp.zeros_like(acc_w)
    for copy, h, low, high in slabs:
        copy.wait()

        @pl.loop(0, rows // SUB)
        def _(b):
            part = rows_of(b)
            accs = [acc_w[part, :]] + [jnp.zeros((SUB, LANES), jnp.float32)] * 3
            for i, t in enumerate(range(low, high)):
                accs[i % 4] = accs[i % 4] + w_ref[h, part, tile(t)]
            acc_w[part, :] = (accs[0] + accs[1]) + (accs[2] + accs[3])

    row_sum = jnp.sum(acc_w[...].T, axis=0, keepdims=True)
    message(msg_ref, row_sum, jnp.zeros((1, LANES), jnp.float32))


def prepare_kernel(
    cid_hbm, cid_row_hbm, goal_row_hbm, tgt_hbm, seg_ref, cols_ref, share_ref, share_row_ref, cid_ref, cid_row, goal_row, tgt_ref, acc_t, sems
):
    copies = [
        pltpu.make_async_copy(cid_hbm, cid_ref, sems.at[0]),
        pltpu.make_async_copy(cid_row_hbm, cid_row, sems.at[1]),
        pltpu.make_async_copy(goal_row_hbm, goal_row, sems.at[2]),
    ]
    for copy in copies:
        copy.start()
    acc_t[...] = jnp.zeros_like(acc_t)
    for copy in copies:
        copy.wait()
    rows = cid_ref.shape[0]
    counties, width = tgt_ref.shape
    tiles = width // LANES
    half = tiles // 2

    low = cid_ref[0] >> 3
    high = (cid_ref[rows - 1] >> 3) + 1

    def targets(b):
        return pltpu.make_async_copy(tgt_hbm.at[rows_of(b)], tgt_ref.at[rows_of(b)], sems.at[3 + b])

    @pl.loop(low, high)
    def _(b):
        targets(b).start()

    n, p, first = 0, 0, 0
    for g in range(rows):
        c = cid_ref[g]
        b = g // SUB
        if g and g % SUB == 0:
            p = p + 1
        seg_ref[pl.ds(n, 1), :] = jnp.full((1, LANES), first + 256 * (b + 1))
        seg_ref[pl.ds(counties + n, 1), :] = jnp.full((1, LANES), c)
        seg_ref[pl.ds(2 * counties + p, 1), :] = jnp.full((1, LANES), b + 256 * n)
        if g + 1 < rows:
            new = cid_ref[g + 1] != c
            step = new.astype(jnp.int32)
            n = n + step
            first = jnp.where(new, (g + 1) // SUB, first)
            if (g + 1) % SUB:
                p = p + step
    last = 2 * counties + PAIRS
    seg_ref[last : last + SUB, :] = jnp.full((SUB, LANES), n + 1 + 256 * (p + 1))
    cols_ref[0] = column(cid_row[...].astype(jnp.float32))
    cols_ref[1] = column(goal_row[...].astype(jnp.float32))

    @pl.loop(low, high)
    def _(b):
        targets(b).wait()
        part = rows_of(b)
        accs = [jnp.zeros((SUB, LANES), jnp.float32)] * 4
        for t in range(tiles):
            accs[t % 4] = accs[t % 4] + tgt_ref[part, tile(t)].astype(jnp.float32)
        acc_t[part, :] = (accs[0] + accs[1]) + (accs[2] + accs[3])

    message(share_row_ref, jnp.zeros((1, LANES), jnp.float32), jnp.sum(acc_t[...].T, axis=0, keepdims=True))

    sub = lax.broadcasted_iota(jnp.int32, (SUB, LANES), 0)
    none = jnp.zeros((SUB, LANES), jnp.float32)

    @pl.loop(0, n + 1)
    def _(k):
        c = seg_name(seg_ref, k)[0, 0]
        part = rows_of(c >> 3)
        mask = sub == (c & 7)
        for h in range(2):
            own = [jnp.where(mask, tgt_ref[part, tile(h * half + t)].astype(jnp.float32) * SHARE, 0.0) for t in range(half)]
            own += [none] * (-half % SUB)
            for t in range(0, len(own), SUB):
                share_ref[k, h, t : t + SUB, :] = fold(own[t : t + SUB])


def side_of(mine):
    core = lax.axis_index("bg") % 2
    return core if mine else 1 - core


def sums_body(second, mine, seg_ref, w_ref, cols_ref, r1_ref, r2_ref, edge_ref, sums_ref, parts_ref):
    w_ref = w_ref.at[side_of(mine)]
    half = w_ref.shape[1] // LANES
    n = seg_counts(seg_ref)[0]
    sub = lax.broadcasted_iota(jnp.int32, (SUB, LANES), 0)
    none = jnp.zeros((SUB, LANES), jnp.float32)

    def county(k, place):
        name = seg_name(seg_ref, k).astype(jnp.float32)

        def block(b, accs):
            rows = rows_of(b)
            mask = cols_ref[0, rows, :] == name
            r1 = jnp.where(mask, r1_ref[rows, :], 0.0)
            out = []
            if second:
                r2 = r2_ref[rows, :]
                for t in range(half):
                    out.append(accs[t] + w_ref[rows, tile(t)] * r1 * r2)
            else:
                for t in range(half):
                    out.append(accs[t] + w_ref[rows, tile(t)] * r1)
                out.append(accs[half] + jnp.where(mask, cols_ref[1, rows, :], 0.0))
            return tuple(out)

        parts = list(lax.fori_loop(place & 255, place >> 8, block, (none,) * (half if second else half + 1)))
        following = seg_number(seg_ref, k + 1)
        if second:
            parts.append(none)
        parts.append(jnp.where(sub == 0, name, 0.0))
        parts += [none] * (-len(parts) % SUB)
        for i, part in enumerate(parts):
            parts_ref[i * SUB : (i + 1) * SUB, :] = part
        for t in range(0, len(parts), SUB):
            folded = [parts_ref[pl.ds(t * SUB + i, SUB, stride=SUB), :] for i in range(SUB)]
            while len(folded) > 1:
                folded = [x + y for x, y in zip(folded[0::2], folded[1::2])]
            sums_ref[k, t : t + SUB, :] = folded[0]
        return following

    lax.fori_loop(0, n, county, seg_number(seg_ref, 0))
    edge_ref[0] = sums_ref[0]
    edge_ref[1] = sums_ref[n - 1]


def give_kernel(second, parts_n, *refs):
    seg_ref, refs = refs[0], refs[1:]
    msgs, refs, parts_ref = refs[:parts_n], refs[parts_n:-1], refs[-1]
    if second:
        w_ref, cols_ref, r1_ref, edge_ref, sums_ref, rcol_ref, total_ref = refs
    else:
        _, w_ref, cols_ref, edge_ref, sums_ref, rcol_ref = refs
        r1_ref = rcol_ref
    total = msgs[0][...]
    for m in msgs[1:]:
        total = total + m[...]
    if second:
        total_ref[...] = total
    rcol = cols_ref[1] / column(total[0:1])
    rcol_ref[...] = rcol * SCALE if second else rcol
    sums_body(second, False, seg_ref, w_ref, cols_ref, r1_ref, rcol_ref, edge_ref, sums_ref, parts_ref)


def keep_kernel(second, seg_ref, w_ref, cols_ref, r1_ref, *refs):
    if not second:
        sums_body(second, True, seg_ref, w_ref, cols_ref, r1_ref, None, *refs)
        return
    r2_ref, total_ref, scale_ref = refs[0], refs[1], refs[4]
    sums_body(second, True, seg_ref, w_ref, cols_ref, r1_ref, r2_ref, refs[2], refs[3], refs[5])
    share = total_ref[1:2, :]
    lane = lax.broadcasted_iota(jnp.int32, (1, LANES), 1)

    @pl.loop(0, (seg_counts(seg_ref)[0] + 3) // 4)
    def _(g):
        for i in range(4):
            k = 4 * g + i
            whole = jnp.sum(jnp.where(lane == seg_name(seg_ref, k), share, 0.0), axis=1, keepdims=True)
            scale_ref[pl.ds(k, 1), :] = jnp.broadcast_to((1.0 / SHARE) / whole, (1, LANES))


def join(refs):
    rows = refs[0].shape[1]
    name = rows - 3
    sub = lax.broadcasted_iota(jnp.int32, (rows, LANES), 0)
    out = []
    for e, pick in ((0, jnp.minimum), (1, jnp.maximum)):
        names = [ref[e, name : name + 1, :] for ref in refs]
        edge = functools.reduce(pick, names)
        total = jnp.zeros((rows, LANES), jnp.float32)
        for ref, own in zip(refs, names):
            total = total + jnp.where(own == edge, ref[e], 0.0)
        out.append(jnp.where(sub == name, edge, total))
    return out


def chip_kernel(keep_ref, got_ref, chip_ref):
    head, tail = join([keep_ref, got_ref])
    chip_ref[0] = head
    chip_ref[1] = tail


def plane_kernel(*refs):
    send_ref = refs[-1]
    z = lax.axis_index("bg") // PLANE
    head, tail = join(refs[:-1])
    for j in range(send_ref.shape[0]):

        @pl.when(j > z)
        def _():
            send_ref[j] = tail

        @pl.when(j <= z)
        def _():
            send_ref[j] = head


def edge_kernel(keep_ref, got_ref, far_ref, *refs):
    chips, (own_ref, other_ref) = refs[:-2], refs[-2:]
    planes, rows = far_ref.shape[:2]
    me = lax.axis_index("bg")
    z = me // PLANE
    x = (me // 2) % (PLANE // 2)
    core = me % 2
    name = rows - 3
    sub = lax.broadcasted_iota(jnp.int32, (rows, LANES), 0)

    for mine_ref, near_ref, out_ref, side in ((keep_ref, got_ref, own_ref, core), (got_ref, keep_ref, other_ref, 1 - core)):
        for e in range(2):
            county = mine_ref[e, name : name + 1, :]
            total = mine_ref[e]

            def add(total, ref, county=county):
                return total + jnp.where(ref[name : name + 1, :] == county, ref[...], 0.0)

            total = add(total, near_ref.at[side])
            for m, chip_ref in enumerate(chips, 1):
                total = add(total, chip_ref.at[jnp.where((x ^ m) < x, 1, 0)])
            for j in range(planes):
                hit = jnp.logical_and(far_ref[j, name : name + 1, :] == county, j != z)
                total = total + jnp.where(hit, far_ref[j], 0.0)
            out_ref[e] = total


def each_sum(n, edge_ref, sums_ref, body):
    group = 4

    @pl.when(n > 2)
    def _():
        @pl.loop(0, (n + group - 1) // group)
        def _(g):
            for i in range(group):
                body(g * group + i, sums_ref.at[g * group + i])

    body(0, edge_ref.at[0])
    body(n - 1, edge_ref.at[1])


def rows_kernel(mine, seg_ref, w_ref, cols_ref, r1_ref, sums_ref, edge_ref, share_ref, *refs):
    if mine:
        goal_ref, acc_ref, fac_ref = refs
    else:
        part_ref, share_row_ref, goal_ref, msg_ref, fac_ref, acc_ref = refs
    w_ref = w_ref.at[side_of(mine)]
    half = w_ref.shape[1] // LANES
    side = side_of(mine)
    n = seg_counts(seg_ref)[0]

    def factor(k, sum_ref):
        goal = share_ref[k, side] * sum_ref[half : half + 1, :]
        goal_ref[k] = goal
        fac_ref[k] = goal / sum_ref[...]

    each_sum(n, edge_ref, sums_ref, factor)
    acc_ref[...] = jnp.zeros_like(acc_ref) if mine else part_ref[...]

    def pair(k, rows, mask):
        r1 = jnp.where(mask, r1_ref[rows, :], 0.0)
        sums = [None] * 4
        for t in range(half):
            x = w_ref[rows, tile(t)] * r1 * fac_ref[k, t : t + 1, :]
            sums[t % 4] = x if sums[t % 4] is None else sums[t % 4] + x
        acc_ref[rows, :] += (sums[0] + sums[1]) + (sums[2] + sums[3])

    each_pair(seg_ref, cols_ref, pair)
    if not mine:
        message(msg_ref, jnp.sum(acc_ref[...].T, axis=0, keepdims=True), share_row_ref[1:2, :])


def fitted(mine, chunks, done, seg_ref, w_ref, cols_ref, r1_ref, r2_ref, goal_ref, scale_ref, sums_ref, edge_ref, out_ref, fac_ref):
    w_ref = w_ref.at[side_of(mine)]
    half = w_ref.shape[1] // LANES
    n = seg_counts(seg_ref)[0]

    def factor(k, sum_ref):
        fac_ref[k] = 100.0 * (goal_ref[k] * scale_ref[pl.ds(k, 1), :] / sum_ref[...])

    each_sum(n, edge_ref, sums_ref, factor)
    for q in range(chunks):
        own = range(q * half // chunks, (q + 1) * half // chunks)

        def pair(k, rows, mask):
            r1 = r1_ref[rows, :]
            r2 = r2_ref[rows, :]
            for t in own:
                x = w_ref[rows, tile(t)] * r1 * r2 * fac_ref[k, t : t + 1, :]
                pltpu.store(out_ref.at[rows, tile(t)], x, mask=mask)

        each_pair(seg_ref, cols_ref, pair)
        done(q)


def last_own_kernel(seg_ref, w_ref, cols_ref, r1_ref, r2_ref, goal_ref, scale_ref, sums_ref, edge_ref, out_ref, fac_ref):
    fitted(True, 1, lambda q: None, seg_ref, w_ref, cols_ref, r1_ref, r2_ref, goal_ref, scale_ref, sums_ref, edge_ref, out_ref, fac_ref)


def last_kernel(
    chunks, seg_ref, w_ref, cols_ref, r1_ref, r2_ref, goal_ref, scale_ref, sums_ref, edge_ref, own_ref, out_hbm, out_ref, fac_ref, sems
):
    width = w_ref.shape[2]
    block = width // chunks

    def place(mine, at, size):
        start = side_of(mine) * width + at
        return out_hbm.at[:, pl.ds(pl.multiple_of(start, LANES), size)]

    copies = []
    for q in range(chunks):
        part = pl.ds(q * block, block)
        copies.append(pltpu.make_async_copy(own_ref.at[:, part], place(True, q * block, block), sems.at[chunks + q]))
        copies[q].start()

    def done(q):
        copy = pltpu.make_async_copy(out_ref.at[:, pl.ds(q * block, block)], place(False, q * block, block), sems.at[q])
        copy.start()
        copies.append(copy)

    fitted(False, chunks, done, seg_ref, w_ref, cols_ref, r1_ref, r2_ref, goal_ref, scale_ref, sums_ref, edge_ref, out_ref, fac_ref)
    for copy in copies:
        copy.wait()


def call(kernel, name, ins, in_specs, out_shape, out_specs=None, scratch=()):
    if out_specs is None:
        out_specs = jax.tree.map(lambda _: VMEM, out_shape)
    return pl.pallas_call(
        kernel,
        out_shape=out_shape,
        in_specs=in_specs,
        out_specs=out_specs,
        scratch_shapes=scratch,
        compiler_params=PARAMS,
        cost_estimate=pl.CostEstimate(flops=4 << 20, bytes_accessed=4 << 20, transcendentals=0),
        name=name,
    )(*ins)


def local(planes, parts, seed_slab, row_target, county_id, county_target):
    rows, width = seed_slab.shape
    counties = county_target.shape[0]
    half = width // LANES // 2
    half_rows = half + 4
    out_chunks = 1
    device = planes * PLANE

    edge = f32(2, half_rows, LANES)
    table = f32(counties, half_rows, LANES)
    column_of = f32(rows, LANES)
    small = f32(SUB, LANES)
    parts_scratch = [pltpu.VMEM((half_rows * SUB, LANES), jnp.float32)]
    inputs = (county_id, county_id.reshape(1, rows), row_target.reshape(1, rows), county_target, seed_slab)
    hbm = [pltpu.with_memory_space_constraint(x, pltpu.HBM) for x in inputs]
    msg, slab = call(
        first_kernel,
        "row_sums_1",
        hbm[4:],
        [HBM],
        (small, f32(2, rows, width // 2)),
        None,
        [pltpu.VMEM((rows, LANES), jnp.float32), pltpu.SemaphoreType.DMA((5,))],
    )

    def swap(x, axis, size, mask):
        return lax.ppermute(x, axis, [(i, i ^ mask) for i in range(size)])

    def over_type(x):
        return [x] + [swap(x, "type", parts, m) for m in range(1, parts)]

    lines = [[PLANE * z + s for z in range(planes)] for s in range(PLANE)]

    def edges(give, keep):
        got = swap(give, "bg", device, 1)
        keep = keep()
        chip = call(chip_kernel, "chip_sums", (keep[0], got), [VMEM] * 2, edge)
        chips = [swap(chip, "bg", device, 2 * m) for m in range(1, PLANE // 2)]
        send = call(plane_kernel, "plane_sums", [chip] + chips, [VMEM] * (PLANE // 2), f32(planes, half_rows, LANES))
        far = lax.all_to_all(send, "bg", 0, 0, axis_index_groups=lines)
        own, other = call(edge_kernel, "edge_sums", [keep[0], got, far] + chips, [VMEM] * (2 + PLANE // 2), (edge, edge))
        return own, swap(other, "bg", device, 1), keep[1:]

    msgs = over_type(msg)
    seg, cols, share, share_row = call(
        prepare_kernel,
        "prepare",
        hbm[:4],
        [HBM] * 4,
        (jax.ShapeDtypeStruct((table_rows(counties), LANES), jnp.int32), f32(2, rows, LANES), f32(counties, 2, half_rows, LANES), small),
        None,
        [
            pltpu.SMEM((rows,), jnp.int32),
            pltpu.VMEM((1, rows), jnp.int32),
            pltpu.VMEM((1, rows), jnp.int32),
            pltpu.VMEM((counties, width), jnp.int32),
            pltpu.VMEM((LANES, LANES), jnp.float32),
            pltpu.SemaphoreType.DMA((3 + counties // SUB,)),
        ],
    )
    give, sums_give, r1 = call(
        functools.partial(give_kernel, False, parts),
        "county_sums_1a",
        [seg] + msgs + [share, slab, cols],
        [VMEM] * (parts + 4),
        (edge, table, column_of),
        None,
        parts_scratch,
    )
    own, other, (sums_keep,) = edges(
        give,
        lambda: call(functools.partial(keep_kernel, False), "county_sums_1b", (seg, slab, cols, r1), [VMEM] * 4, (edge, table), None, parts_scratch),
    )
    fac = pltpu.VMEM((counties, half_rows, LANES), jnp.float32)
    goal_keep, part = call(
        functools.partial(rows_kernel, True),
        "row_sums_2a",
        (seg, slab, cols, r1, sums_keep, own, share),
        [VMEM] * 7,
        (table, column_of),
        None,
        [fac],
    )
    goal_give, msg = call(
        functools.partial(rows_kernel, False),
        "row_sums_2b",
        (seg, slab, cols, r1, sums_give, other, share, part, share_row),
        [VMEM] * 9,
        (table, small),
        None,
        [fac, pltpu.VMEM((rows, LANES), jnp.float32)],
    )
    give, sums_give, r2, total = call(
        functools.partial(give_kernel, True, parts),
        "county_sums_2a",
        [seg] + over_type(msg) + [slab, cols, r1],
        [VMEM] * (parts + 4),
        (edge, table, column_of, small),
        None,
        parts_scratch,
    )
    own, other, (sums_keep, scale) = edges(
        give,
        lambda: call(functools.partial(keep_kernel, True), "county_sums_2b", (seg, slab, cols, r1, r2, total), [VMEM] * 6, (edge, table, f32(counties, LANES)), None, parts_scratch),
    )
    mine = call(
        last_own_kernel,
        "fitted_a",
        (seg, slab, cols, r1, r2, goal_keep, scale, sums_keep, own),
        [VMEM] * 9,
        f32(rows, width // 2),
        None,
        [fac],
    )
    return call(
        functools.partial(last_kernel, out_chunks),
        "fitted_b",
        (seg, slab, cols, r1, r2, goal_give, scale, sums_give, other, mine),
        [VMEM] * 10,
        f32(rows, width),
        HBM,
        [pltpu.VMEM((rows, width // 2), jnp.float32), fac, pltpu.SemaphoreType.DMA((2 * out_chunks,))],
    )


def solution(mesh):
    return jax.shard_map(
        functools.partial(local, mesh.shape["bg"] // PLANE, mesh.shape["type"]),
        mesh=mesh,
        in_specs=(P("bg", "type"), P("bg"), P("bg"), P(None, "type")),
        out_specs=P("bg", "type"),
        check_vma=False,
    )
```

```python
import functools

import jax
import jax.numpy as jnp
from jax import lax
from jax.experimental import pallas as pl
from jax.experimental.pallas import tpu as pltpu
from jax.sharding import PartitionSpec as P

LANES = 128
SUB = 8
PLANE = 8
SCALE = 2.0**30
SHARE = 2.0**-26
VMEM = pl.BlockSpec(memory_space=pltpu.VMEM)
HBM = pl.BlockSpec(memory_space=pltpu.HBM)
PARAMS = pltpu.CompilerParams(vmem_limit_bytes=32 * 1024 * 1024)


def f32(*shape):
    return jax.ShapeDtypeStruct(shape, jnp.float32)


def tile(t):
    return pl.ds(t * LANES, LANES)


def rows_of(b):
    return pl.ds(pl.multiple_of(b * SUB, SUB), SUB)


def column(row):
    return jnp.broadcast_to(row, (LANES, LANES)).T


def fold(parts):
    sub = lax.broadcasted_iota(jnp.int32, (SUB, LANES), 0)
    order, step = list(parts), 1
    while step < SUB:
        mask = (sub & step) == 0
        merged = []
        for a, b in zip(order[0::2], order[1::2]):
            merged.append(jnp.where(mask, a, b) + pltpu.roll(jnp.where(mask, b, a), SUB - step, 0))
        order, step = merged, 2 * step
    return order[0]


PAIRS = 80


def table_rows(counties):
    return 2 * counties + PAIRS + SUB


def seg_number(seg_ref, row):
    return seg_ref[pl.ds(row, 1), :][0, 0]


def seg_counties(seg_ref):
    return (seg_ref.shape[0] - SUB - PAIRS) // 2


def seg_counts(seg_ref):
    both = seg_number(seg_ref, seg_ref.shape[0] - SUB)
    return both & 255, both >> 8


def seg_name(seg_ref, k):
    return seg_ref[pl.ds(seg_counties(seg_ref) + k, 1), :]


def each_pair(seg_ref, cols_ref, body):
    at = 2 * seg_counties(seg_ref)

    def step(p, pair):
        following = seg_number(seg_ref, at + p + 1)
        k = pair >> 8
        rows = rows_of(pair & 255)
        mask = cols_ref[0, rows, :] == seg_name(seg_ref, k).astype(jnp.float32)
        body(k, rows, mask)
        return following

    lax.fori_loop(0, seg_counts(seg_ref)[1], step, seg_number(seg_ref, at))


def message(msg_ref, row_sum, share):
    sub = lax.broadcasted_iota(jnp.int32, (SUB, LANES), 0)
    msg_ref[...] = jnp.where(sub == 0, row_sum, jnp.where(sub == 1, share, 0.0))


def first_kernel(w_hbm, msg_ref, w_ref, acc_w, sems):
    rows, half = w_ref.shape[1:]
    tiles = half // LANES
    cuts = [[0, tiles // 2, tiles], [0, tiles // 2, 5 * tiles // 6, tiles]]
    slabs = []
    for h, cut in enumerate(cuts):
        for low, high in zip(cut, cut[1:]):
            size = (high - low) * LANES
            from_hbm = w_hbm.at[:, pl.ds(h * half + low * LANES, size)]
            copy = pltpu.make_async_copy(from_hbm, w_ref.at[h, :, pl.ds(low * LANES, size)], sems.at[len(slabs)])
            copy.start()
            slabs.append((copy, h, low, high))
    acc_w[...] = jnp.zeros_like(acc_w)
    for copy, h, low, high in slabs:
        copy.wait()

        @pl.loop(0, rows // SUB)
        def _(b):
            part = rows_of(b)
            accs = [acc_w[part, :]] + [jnp.zeros((SUB, LANES), jnp.float32)] * 3
            for i, t in enumerate(range(low, high)):
                accs[i % 4] = accs[i % 4] + w_ref[h, part, tile(t)]
            acc_w[part, :] = (accs[0] + accs[1]) + (accs[2] + accs[3])

    row_sum = jnp.sum(acc_w[...].T, axis=0, keepdims=True)
    message(msg_ref, row_sum, jnp.zeros((1, LANES), jnp.float32))


def prepare_kernel(
    cid_hbm, cid_row_hbm, goal_row_hbm, tgt_hbm, seg_ref, cols_ref, share_ref, share_row_ref, cid_ref, cid_row, goal_row, tgt_ref, acc_t, sems
):
    copies = [
        pltpu.make_async_copy(cid_hbm, cid_ref, sems.at[0]),
        pltpu.make_async_copy(cid_row_hbm, cid_row, sems.at[1]),
        pltpu.make_async_copy(goal_row_hbm, goal_row, sems.at[2]),
    ]
    for copy in copies:
        copy.start()
    acc_t[...] = jnp.zeros_like(acc_t)
    for copy in copies:
        copy.wait()
    rows = cid_ref.shape[0]
    counties, width = tgt_ref.shape
    tiles = width // LANES
    half = tiles // 2

    low = cid_ref[0] >> 3
    high = (cid_ref[rows - 1] >> 3) + 1

    def targets(b):
        return pltpu.make_async_copy(tgt_hbm.at[rows_of(b)], tgt_ref.at[rows_of(b)], sems.at[3 + b])

    @pl.loop(low, high)
    def _(b):
        targets(b).start()

    n, p, first = 0, 0, 0
    for g in range(rows):
        c = cid_ref[g]
        b = g // SUB
        if g and g % SUB == 0:
            p = p + 1
        seg_ref[pl.ds(n, 1), :] = jnp.full((1, LANES), first + 256 * (b + 1))
        seg_ref[pl.ds(counties + n, 1), :] = jnp.full((1, LANES), c)
        seg_ref[pl.ds(2 * counties + p, 1), :] = jnp.full((1, LANES), b + 256 * n)
        if g + 1 < rows:
            new = cid_ref[g + 1] != c
            step = new.astype(jnp.int32)
            n = n + step
            first = jnp.where(new, (g + 1) // SUB, first)
            if (g + 1) % SUB:
                p = p + step
    last = 2 * counties + PAIRS
    seg_ref[last : last + SUB, :] = jnp.full((SUB, LANES), n + 1 + 256 * (p + 1))
    cols_ref[0] = column(cid_row[...].astype(jnp.float32))
    cols_ref[1] = column(goal_row[...].astype(jnp.float32))

    @pl.loop(low, high)
    def _(b):
        targets(b).wait()
        part = rows_of(b)
        accs = [jnp.zeros((SUB, LANES), jnp.float32)] * 4
        for t in range(tiles):
            accs[t % 4] = accs[t % 4] + tgt_ref[part, tile(t)].astype(jnp.float32)
        acc_t[part, :] = (accs[0] + accs[1]) + (accs[2] + accs[3])

    message(share_row_ref, jnp.zeros((1, LANES), jnp.float32), jnp.sum(acc_t[...].T, axis=0, keepdims=True))

    sub = lax.broadcasted_iota(jnp.int32, (SUB, LANES), 0)
    none = jnp.zeros((SUB, LANES), jnp.float32)

    @pl.loop(0, n + 1)
    def _(k):
        c = seg_name(seg_ref, k)[0, 0]
        part = rows_of(c >> 3)
        mask = sub == (c & 7)
        for h in range(2):
            own = [jnp.where(mask, tgt_ref[part, tile(h * half + t)].astype(jnp.float32) * SHARE, 0.0) for t in range(half)]
            own += [none] * (-half % SUB)
            for t in range(0, len(own), SUB):
                share_ref[k, h, t : t + SUB, :] = fold(own[t : t + SUB])


def side_of(mine):
    core = lax.axis_index("bg") % 2
    return core if mine else 1 - core


def sums_body(second, mine, ends, seg_ref, w_ref, cols_ref, r1_ref, r2_ref, sums_ref, parts_ref):
    w_ref = w_ref.at[side_of(mine)]
    half = w_ref.shape[1] // LANES
    n = seg_counts(seg_ref)[0]
    sub = lax.broadcasted_iota(jnp.int32, (SUB, LANES), 0)
    none = jnp.zeros((SUB, LANES), jnp.float32)

    def county(at, place):
        k = at * (n - 1) if ends else at
        name = seg_name(seg_ref, k).astype(jnp.float32)

        def block(b, accs):
            rows = rows_of(b)
            mask = cols_ref[0, rows, :] == name
            r1 = jnp.where(mask, r1_ref[rows, :], 0.0)
            out = []
            if second:
                r2 = r2_ref[rows, :]
                for t in range(half):
                    out.append(accs[t] + w_ref[rows, tile(t)] * r1 * r2)
            else:
                for t in range(half):
                    out.append(accs[t] + w_ref[rows, tile(t)] * r1)
                out.append(accs[half] + jnp.where(mask, cols_ref[1, rows, :], 0.0))
            return tuple(out)

        parts = list(lax.fori_loop(place & 255, place >> 8, block, (none,) * (half if second else half + 1)))
        following = seg_number(seg_ref, n - 1 if ends else k + 1)
        if second:
            parts.append(none)
        parts.append(jnp.where(sub == 0, name, 0.0))
        parts += [none] * (-len(parts) % SUB)
        for i, part in enumerate(parts):
            parts_ref[i * SUB : (i + 1) * SUB, :] = part
        for t in range(0, len(parts), SUB):
            folded = [parts_ref[pl.ds(t * SUB + i, SUB, stride=SUB), :] for i in range(SUB)]
            while len(folded) > 1:
                folded = [x + y for x, y in zip(folded[0::2], folded[1::2])]
            sums_ref[at, t : t + SUB, :] = folded[0]
        return following

    if ends:
        lax.fori_loop(0, jnp.minimum(n, 2), county, seg_number(seg_ref, 0))

        @pl.when(n == 1)
        def _():
            sums_ref[1] = sums_ref[0]

    else:
        lax.fori_loop(1, n - 1, county, seg_number(seg_ref, 1))


def give_kernel(second, parts_n, *refs):
    seg_ref, refs = refs[0], refs[1:]
    msgs, refs, parts_ref = refs[:parts_n], refs[parts_n:-1], refs[-1]
    if second:
        w_ref, cols_ref, r1_ref, edge_ref, rcol_ref, total_ref = refs
    else:
        _, w_ref, cols_ref, edge_ref, rcol_ref = refs
        r1_ref = rcol_ref
    total = msgs[0][...]
    for m in msgs[1:]:
        total = total + m[...]
    if second:
        total_ref[...] = total
    rcol = cols_ref[1] / column(total[0:1])
    rcol_ref[...] = rcol * SCALE if second else rcol
    sums_body(second, False, True, seg_ref, w_ref, cols_ref, r1_ref, rcol_ref, edge_ref, parts_ref)


def keep_kernel(second, seg_ref, w_ref, cols_ref, r1_ref, *refs):
    if second:
        r2_ref, total_ref, edge_ref, sums_ref, scale_ref, give_ref, parts_ref = refs
    else:
        edge_ref, sums_ref, give_ref, parts_ref = refs
        r2_ref = None
    for mine, ends, out_ref in ((True, True, edge_ref), (True, False, sums_ref), (False, False, give_ref)):
        sums_body(second, mine, ends, seg_ref, w_ref, cols_ref, r1_ref, r2_ref, out_ref, parts_ref)
    if not second:
        return
    share = total_ref[1:2, :]
    lane = lax.broadcasted_iota(jnp.int32, (1, LANES), 1)

    @pl.loop(0, (seg_counts(seg_ref)[0] + 3) // 4)
    def _(g):
        for i in range(4):
            k = 4 * g + i
            whole = jnp.sum(jnp.where(lane == seg_name(seg_ref, k), share, 0.0), axis=1, keepdims=True)
            scale_ref[pl.ds(k, 1), :] = jnp.broadcast_to((1.0 / SHARE) / whole, (1, LANES))


def join(refs):
    rows = refs[0].shape[1]
    name = rows - 3
    sub = lax.broadcasted_iota(jnp.int32, (rows, LANES), 0)
    out = []
    for e, pick in ((0, jnp.minimum), (1, jnp.maximum)):
        names = [ref[e, name : name + 1, :] for ref in refs]
        edge = functools.reduce(pick, names)
        total = jnp.zeros((rows, LANES), jnp.float32)
        for ref, own in zip(refs, names):
            total = total + jnp.where(own == edge, ref[e], 0.0)
        out.append(jnp.where(sub == name, edge, total))
    return out


def chip_kernel(keep_ref, got_ref, chip_ref):
    head, tail = join([keep_ref, got_ref])
    chip_ref[0] = head
    chip_ref[1] = tail


def plane_kernel(*refs):
    send_ref = refs[-1]
    z = lax.axis_index("bg") // PLANE
    head, tail = join(refs[:-1])
    for j in range(send_ref.shape[0]):

        @pl.when(j > z)
        def _():
            send_ref[j] = tail

        @pl.when(j <= z)
        def _():
            send_ref[j] = head


def edge_kernel(keep_ref, got_ref, far_ref, *refs):
    chips, (own_ref, other_ref) = refs[:-2], refs[-2:]
    planes, rows = far_ref.shape[:2]
    me = lax.axis_index("bg")
    z = me // PLANE
    x = (me // 2) % (PLANE // 2)
    core = me % 2
    name = rows - 3
    sub = lax.broadcasted_iota(jnp.int32, (rows, LANES), 0)

    for mine_ref, near_ref, out_ref, side in ((keep_ref, got_ref, own_ref, core), (got_ref, keep_ref, other_ref, 1 - core)):
        for e in range(2):
            county = mine_ref[e, name : name + 1, :]
            total = mine_ref[e]

            def add(total, ref, county=county):
                return total + jnp.where(ref[name : name + 1, :] == county, ref[...], 0.0)

            total = add(total, near_ref.at[side])
            for m, chip_ref in enumerate(chips, 1):
                total = add(total, chip_ref.at[jnp.where((x ^ m) < x, 1, 0)])
            for j in range(planes):
                hit = jnp.logical_and(far_ref[j, name : name + 1, :] == county, j != z)
                total = total + jnp.where(hit, far_ref[j], 0.0)
            out_ref[e] = total


def each_sum(n, edge_ref, sums_ref, body):
    group = 4

    @pl.when(n > 2)
    def _():
        @pl.loop(0, (n + group - 1) // group)
        def _(g):
            for i in range(group):
                body(g * group + i, sums_ref.at[g * group + i])

    body(0, edge_ref.at[0])
    body(n - 1, edge_ref.at[1])


def rows_kernel(mine, seg_ref, w_ref, cols_ref, r1_ref, sums_ref, edge_ref, share_ref, *refs):
    if mine:
        goal_ref, acc_ref, fac_ref = refs
    else:
        part_ref, share_row_ref, goal_ref, msg_ref, fac_ref, acc_ref = refs
    w_ref = w_ref.at[side_of(mine)]
    half = w_ref.shape[1] // LANES
    side = side_of(mine)
    n = seg_counts(seg_ref)[0]

    def factor(k, sum_ref):
        goal = share_ref[k, side] * sum_ref[half : half + 1, :]
        goal_ref[k] = goal
        fac_ref[k] = goal / sum_ref[...]

    each_sum(n, edge_ref, sums_ref, factor)
    acc_ref[...] = jnp.zeros_like(acc_ref) if mine else part_ref[...]

    def pair(k, rows, mask):
        r1 = jnp.where(mask, r1_ref[rows, :], 0.0)
        sums = [None] * 4
        for t in range(half):
            x = w_ref[rows, tile(t)] * r1 * fac_ref[k, t : t + 1, :]
            sums[t % 4] = x if sums[t % 4] is None else sums[t % 4] + x
        acc_ref[rows, :] += (sums[0] + sums[1]) + (sums[2] + sums[3])

    each_pair(seg_ref, cols_ref, pair)
    if not mine:
        message(msg_ref, jnp.sum(acc_ref[...].T, axis=0, keepdims=True), share_row_ref[1:2, :])


def fitted(mine, chunks, done, seg_ref, w_ref, cols_ref, r1_ref, r2_ref, goal_ref, scale_ref, sums_ref, edge_ref, out_ref, fac_ref):
    w_ref = w_ref.at[side_of(mine)]
    half = w_ref.shape[1] // LANES
    n = seg_counts(seg_ref)[0]

    def factor(k, sum_ref):
        fac_ref[k] = 100.0 * (goal_ref[k] * scale_ref[pl.ds(k, 1), :] / sum_ref[...])

    each_sum(n, edge_ref, sums_ref, factor)
    for q in range(chunks):
        own = range(q * half // chunks, (q + 1) * half // chunks)

        def pair(k, rows, mask):
            r1 = r1_ref[rows, :]
            r2 = r2_ref[rows, :]
            for t in own:
                x = w_ref[rows, tile(t)] * r1 * r2 * fac_ref[k, t : t + 1, :]
                pltpu.store(out_ref.at[rows, tile(t)], x, mask=mask)

        each_pair(seg_ref, cols_ref, pair)
        done(q)


def last_own_kernel(seg_ref, w_ref, cols_ref, r1_ref, r2_ref, goal_ref, scale_ref, sums_ref, edge_ref, out_ref, fac_ref):
    fitted(True, 1, lambda q: None, seg_ref, w_ref, cols_ref, r1_ref, r2_ref, goal_ref, scale_ref, sums_ref, edge_ref, out_ref, fac_ref)


def last_kernel(
    chunks, seg_ref, w_ref, cols_ref, r1_ref, r2_ref, goal_ref, scale_ref, sums_ref, edge_ref, own_ref, out_hbm, out_ref, fac_ref, sems
):
    width = w_ref.shape[2]
    block = width // chunks

    def place(mine, at, size):
        start = side_of(mine) * width + at
        return out_hbm.at[:, pl.ds(pl.multiple_of(start, LANES), size)]

    copies = []
    for q in range(chunks):
        part = pl.ds(q * block, block)
        copies.append(pltpu.make_async_copy(own_ref.at[:, part], place(True, q * block, block), sems.at[chunks + q]))
        copies[q].start()

    def done(q):
        copy = pltpu.make_async_copy(out_ref.at[:, pl.ds(q * block, block)], place(False, q * block, block), sems.at[q])
        copy.start()
        copies.append(copy)

    fitted(False, chunks, done, seg_ref, w_ref, cols_ref, r1_ref, r2_ref, goal_ref, scale_ref, sums_ref, edge_ref, out_ref, fac_ref)
    for copy in copies:
        copy.wait()


def call(kernel, name, ins, in_specs, out_shape, out_specs=None, scratch=()):
    if out_specs is None:
        out_specs = jax.tree.map(lambda _: VMEM, out_shape)
    return pl.pallas_call(
        kernel,
        out_shape=out_shape,
        in_specs=in_specs,
        out_specs=out_specs,
        scratch_shapes=scratch,
        compiler_params=PARAMS,
        cost_estimate=pl.CostEstimate(flops=4 << 20, bytes_accessed=4 << 20, transcendentals=0),
        name=name,
    )(*ins)


def local(planes, parts, seed_slab, row_target, county_id, county_target):
    rows, width = seed_slab.shape
    counties = county_target.shape[0]
    half = width // LANES // 2
    half_rows = half + 4
    out_chunks = 1
    device = planes * PLANE

    edge = f32(2, half_rows, LANES)
    table = f32(counties, half_rows, LANES)
    column_of = f32(rows, LANES)
    small = f32(SUB, LANES)
    parts_scratch = [pltpu.VMEM((half_rows * SUB, LANES), jnp.float32)]
    inputs = (county_id, county_id.reshape(1, rows), row_target.reshape(1, rows), county_target, seed_slab)
    hbm = [pltpu.with_memory_space_constraint(x, pltpu.HBM) for x in inputs]
    msg, slab = call(
        first_kernel,
        "row_sums_1",
        hbm[4:],
        [HBM],
        (small, f32(2, rows, width // 2)),
        None,
        [pltpu.VMEM((rows, LANES), jnp.float32), pltpu.SemaphoreType.DMA((5,))],
    )

    def swap(x, axis, size, mask):
        return lax.ppermute(x, axis, [(i, i ^ mask) for i in range(size)])

    def over_type(x):
        return [x] + [swap(x, "type", parts, m) for m in range(1, parts)]

    lines = [[PLANE * z + s for z in range(planes)] for s in range(PLANE)]

    def edges(give, keep):
        got = swap(give, "bg", device, 1)
        keep = keep()
        chip = call(chip_kernel, "chip_sums", (keep[0], got), [VMEM] * 2, edge)
        chips = [swap(chip, "bg", device, 2 * m) for m in range(1, PLANE // 2)]
        send = call(plane_kernel, "plane_sums", [chip] + chips, [VMEM] * (PLANE // 2), f32(planes, half_rows, LANES))
        far = lax.all_to_all(send, "bg", 0, 0, axis_index_groups=lines)
        own, other = call(edge_kernel, "edge_sums", [keep[0], got, far] + chips, [VMEM] * (2 + PLANE // 2), (edge, edge))
        return own, swap(other, "bg", device, 1), keep[1:]

    msgs = over_type(msg)
    seg, cols, share, share_row = call(
        prepare_kernel,
        "prepare",
        hbm[:4],
        [HBM] * 4,
        (jax.ShapeDtypeStruct((table_rows(counties), LANES), jnp.int32), f32(2, rows, LANES), f32(counties, 2, half_rows, LANES), small),
        None,
        [
            pltpu.SMEM((rows,), jnp.int32),
            pltpu.VMEM((1, rows), jnp.int32),
            pltpu.VMEM((1, rows), jnp.int32),
            pltpu.VMEM((counties, width), jnp.int32),
            pltpu.VMEM((LANES, LANES), jnp.float32),
            pltpu.SemaphoreType.DMA((3 + counties // SUB,)),
        ],
    )
    give, r1 = call(
        functools.partial(give_kernel, False, parts),
        "county_sums_1a",
        [seg] + msgs + [share, slab, cols],
        [VMEM] * (parts + 4),
        (edge, column_of),
        None,
        parts_scratch,
    )
    own, other, (sums_keep, sums_give) = edges(
        give,
        lambda: call(functools.partial(keep_kernel, False), "county_sums_1b", (seg, slab, cols, r1), [VMEM] * 4, (edge, table, table), None, parts_scratch),
    )
    fac = pltpu.VMEM((counties, half_rows, LANES), jnp.float32)
    goal_keep, part = call(
        functools.partial(rows_kernel, True),
        "row_sums_2a",
        (seg, slab, cols, r1, sums_keep, own, share),
        [VMEM] * 7,
        (table, column_of),
        None,
        [fac],
    )
    goal_give, msg = call(
        functools.partial(rows_kernel, False),
        "row_sums_2b",
        (seg, slab, cols, r1, sums_give, other, share, part, share_row),
        [VMEM] * 9,
        (table, small),
        None,
        [fac, pltpu.VMEM((rows, LANES), jnp.float32)],
    )
    give, r2, total = call(
        functools.partial(give_kernel, True, parts),
        "county_sums_2a",
        [seg] + over_type(msg) + [slab, cols, r1],
        [VMEM] * (parts + 4),
        (edge, column_of, small),
        None,
        parts_scratch,
    )
    own, other, (sums_keep, scale, sums_give) = edges(
        give,
        lambda: call(functools.partial(keep_kernel, True), "county_sums_2b", (seg, slab, cols, r1, r2, total), [VMEM] * 6, (edge, table, f32(counties, LANES), table), None, parts_scratch),
    )
    mine = call(
        last_own_kernel,
        "fitted_a",
        (seg, slab, cols, r1, r2, goal_keep, scale, sums_keep, own),
        [VMEM] * 9,
        f32(rows, width // 2),
        None,
        [fac],
    )
    return call(
        functools.partial(last_kernel, out_chunks),
        "fitted_b",
        (seg, slab, cols, r1, r2, goal_give, scale, sums_give, other, mine),
        [VMEM] * 10,
        f32(rows, width),
        HBM,
        [pltpu.VMEM((rows, width // 2), jnp.float32), fac, pltpu.SemaphoreType.DMA((2 * out_chunks,))],
    )


def solution(mesh):
    return jax.shard_map(
        functools.partial(local, mesh.shape["bg"] // PLANE, mesh.shape["type"]),
        mesh=mesh,
        in_specs=(P("bg", "type"), P("bg"), P("bg"), P(None, "type")),
        out_specs=P("bg", "type"),
        check_vma=False,
    )
```

```python
import functools

import jax
import jax.numpy as jnp
from jax import lax
from jax.experimental import pallas as pl
from jax.experimental.pallas import tpu as pltpu
from jax.sharding import PartitionSpec as P

LANES = 128
SUB = 8
PLANE = 8
SCALE = 2.0**30
SHARE = 2.0**-26
VMEM = pl.BlockSpec(memory_space=pltpu.VMEM)
HBM = pl.BlockSpec(memory_space=pltpu.HBM)
PARAMS = pltpu.CompilerParams(vmem_limit_bytes=32 * 1024 * 1024)


def f32(*shape):
    return jax.ShapeDtypeStruct(shape, jnp.float32)


def tile(t):
    return pl.ds(t * LANES, LANES)


def rows_of(b):
    return pl.ds(pl.multiple_of(b * SUB, SUB), SUB)


def column(row):
    return jnp.broadcast_to(row, (LANES, LANES)).T


def fold(parts):
    sub = lax.broadcasted_iota(jnp.int32, (SUB, LANES), 0)
    order, step = list(parts), 1
    while step < SUB:
        mask = (sub & step) == 0
        merged = []
        for a, b in zip(order[0::2], order[1::2]):
            merged.append(jnp.where(mask, a, b) + pltpu.roll(jnp.where(mask, b, a), SUB - step, 0))
        order, step = merged, 2 * step
    return order[0]


PAIRS = 80


def table_rows(counties):
    return 2 * counties + PAIRS + SUB


def seg_number(seg_ref, row):
    return seg_ref[pl.ds(row, 1), :][0, 0]


def seg_counties(seg_ref):
    return (seg_ref.shape[0] - SUB - PAIRS) // 2


def seg_counts(seg_ref):
    both = seg_number(seg_ref, seg_ref.shape[0] - SUB)
    return both & 255, both >> 8


def seg_name(seg_ref, k):
    return seg_ref[pl.ds(seg_counties(seg_ref) + k, 1), :]


def each_pair(seg_ref, cols_ref, body):
    at = 2 * seg_counties(seg_ref)

    def step(p, pair):
        following = seg_number(seg_ref, at + p + 1)
        k = pair >> 8
        rows = rows_of(pair & 255)
        mask = cols_ref[0, rows, :] == seg_name(seg_ref, k).astype(jnp.float32)
        body(k, rows, mask)
        return following

    lax.fori_loop(0, seg_counts(seg_ref)[1], step, seg_number(seg_ref, at))


def message(msg_ref, row_sum, share):
    sub = lax.broadcasted_iota(jnp.int32, (SUB, LANES), 0)
    msg_ref[...] = jnp.where(sub == 0, row_sum, jnp.where(sub == 1, share, 0.0))


def first_kernel(w_hbm, msg_ref, w_ref, acc_w, sems):
    rows, half = w_ref.shape[1:]
    tiles = half // LANES
    cuts = [[0, tiles // 2, tiles], [0, tiles // 2, 5 * tiles // 6, tiles]]
    slabs = []
    for h, cut in enumerate(cuts):
        for low, high in zip(cut, cut[1:]):
            size = (high - low) * LANES
            from_hbm = w_hbm.at[:, pl.ds(h * half + low * LANES, size)]
            copy = pltpu.make_async_copy(from_hbm, w_ref.at[h, :, pl.ds(low * LANES, size)], sems.at[len(slabs)])
            copy.start()
            slabs.append((copy, h, low, high))
    acc_w[...] = jnp.zeros_like(acc_w)
    for copy, h, low, high in slabs:
        copy.wait()

        @pl.loop(0, rows // SUB)
        def _(b):
            part = rows_of(b)
            accs = [acc_w[part, :]] + [jnp.zeros((SUB, LANES), jnp.float32)] * 3
            for i, t in enumerate(range(low, high)):
                accs[i % 4] = accs[i % 4] + w_ref[h, part, tile(t)]
            acc_w[part, :] = (accs[0] + accs[1]) + (accs[2] + accs[3])

    row_sum = jnp.sum(acc_w[...].T, axis=0, keepdims=True)
    message(msg_ref, row_sum, jnp.zeros((1, LANES), jnp.float32))


def prepare_kernel(
    cid_hbm, cid_row_hbm, goal_row_hbm, tgt_hbm, seg_ref, cols_ref, share_ref, share_row_ref, cid_ref, cid_row, goal_row, tgt_ref, acc_t, sems
):
    copies = [
        pltpu.make_async_copy(cid_hbm, cid_ref, sems.at[0]),
        pltpu.make_async_copy(cid_row_hbm, cid_row, sems.at[1]),
        pltpu.make_async_copy(goal_row_hbm, goal_row, sems.at[2]),
    ]
    for copy in copies:
        copy.start()
    acc_t[...] = jnp.zeros_like(acc_t)
    for copy in copies:
        copy.wait()
    rows = cid_ref.shape[0]
    counties, width = tgt_ref.shape
    tiles = width // LANES
    half = tiles // 2

    low = cid_ref[0] >> 3
    high = (cid_ref[rows - 1] >> 3) + 1

    def targets(b):
        return pltpu.make_async_copy(tgt_hbm.at[rows_of(b)], tgt_ref.at[rows_of(b)], sems.at[3 + b])

    @pl.loop(low, high)
    def _(b):
        targets(b).start()

    n, p, first = 0, 0, 0
    for g in range(rows):
        c = cid_ref[g]
        b = g // SUB
        if g and g % SUB == 0:
            p = p + 1
        seg_ref[pl.ds(n, 1), :] = jnp.full((1, LANES), first + 256 * (b + 1))
        seg_ref[pl.ds(counties + n, 1), :] = jnp.full((1, LANES), c)
        seg_ref[pl.ds(2 * counties + p, 1), :] = jnp.full((1, LANES), b + 256 * n)
        if g + 1 < rows:
            new = cid_ref[g + 1] != c
            step = new.astype(jnp.int32)
            n = n + step
            first = jnp.where(new, (g + 1) // SUB, first)
            if (g + 1) % SUB:
                p = p + step
    last = 2 * counties + PAIRS
    seg_ref[last : last + SUB, :] = jnp.full((SUB, LANES), n + 1 + 256 * (p + 1))
    cols_ref[0] = column(cid_row[...].astype(jnp.float32))
    cols_ref[1] = column(goal_row[...].astype(jnp.float32))

    @pl.loop(low, high)
    def _(b):
        targets(b).wait()
        part = rows_of(b)
        accs = [jnp.zeros((SUB, LANES), jnp.float32)] * 4
        for t in range(tiles):
            accs[t % 4] = accs[t % 4] + tgt_ref[part, tile(t)].astype(jnp.float32)
        acc_t[part, :] = (accs[0] + accs[1]) + (accs[2] + accs[3])

    message(share_row_ref, jnp.zeros((1, LANES), jnp.float32), jnp.sum(acc_t[...].T, axis=0, keepdims=True))

    sub = lax.broadcasted_iota(jnp.int32, (SUB, LANES), 0)
    none = jnp.zeros((SUB, LANES), jnp.float32)

    @pl.loop(0, n + 1)
    def _(k):
        c = seg_name(seg_ref, k)[0, 0]
        part = rows_of(c >> 3)
        mask = sub == (c & 7)
        for h in range(2):
            own = [jnp.where(mask, tgt_ref[part, tile(h * half + t)].astype(jnp.float32) * SHARE, 0.0) for t in range(half)]
            own += [none] * (-half % SUB)
            for t in range(0, len(own), SUB):
                share_ref[k, h, t : t + SUB, :] = fold(own[t : t + SUB])


def side_of(mine):
    core = lax.axis_index("bg") % 2
    return core if mine else 1 - core


def sums_body(second, mine, ends, seg_ref, w_ref, cols_ref, r1_ref, r2_ref, sums_ref, parts_ref):
    w_ref = w_ref.at[side_of(mine)]
    half = w_ref.shape[1] // LANES
    n = seg_counts(seg_ref)[0]
    sub = lax.broadcasted_iota(jnp.int32, (SUB, LANES), 0)
    none = jnp.zeros((SUB, LANES), jnp.float32)

    def county(at, place):
        k = at * (n - 1) if ends else at
        name = seg_name(seg_ref, k).astype(jnp.float32)

        def block(b, accs):
            rows = rows_of(b)
            mask = cols_ref[0, rows, :] == name
            r1 = jnp.where(mask, r1_ref[rows, :], 0.0)
            out = []
            if second:
                r2 = r2_ref[rows, :]
                for t in range(half):
                    out.append(accs[t] + w_ref[rows, tile(t)] * r1 * r2)
            else:
                for t in range(half):
                    out.append(accs[t] + w_ref[rows, tile(t)] * r1)
                out.append(accs[half] + jnp.where(mask, cols_ref[1, rows, :], 0.0))
            return tuple(out)

        parts = list(lax.fori_loop(place & 255, place >> 8, block, (none,) * (half if second else half + 1)))
        following = seg_number(seg_ref, n - 1 if ends else k + 1)
        if second:
            parts.append(none)
        parts.append(jnp.where(sub == 0, name, 0.0))
        parts += [none] * (-len(parts) % SUB)
        for i, part in enumerate(parts):
            parts_ref[i * SUB : (i + 1) * SUB, :] = part
        for t in range(0, len(parts), SUB):
            folded = [parts_ref[pl.ds(t * SUB + i, SUB, stride=SUB), :] for i in range(SUB)]
            while len(folded) > 1:
                folded = [x + y for x, y in zip(folded[0::2], folded[1::2])]
            sums_ref[at, t : t + SUB, :] = folded[0]
        return following

    if ends:
        lax.fori_loop(0, jnp.minimum(n, 2), county, seg_number(seg_ref, 0))

        @pl.when(n == 1)
        def _():
            sums_ref[1] = sums_ref[0]

    else:
        lax.fori_loop(1, n - 1, county, seg_number(seg_ref, 1))


def give_kernel(second, parts_n, *refs):
    seg_ref, refs = refs[0], refs[1:]
    msgs, refs, parts_ref = refs[:parts_n], refs[parts_n:-1], refs[-1]
    if second:
        w_ref, cols_ref, r1_ref, edge_ref, rcol_ref, total_ref = refs
    else:
        _, w_ref, cols_ref, edge_ref, rcol_ref = refs
        r1_ref = rcol_ref
    total = msgs[0][...]
    for m in msgs[1:]:
        total = total + m[...]
    if second:
        total_ref[...] = total
    rcol = cols_ref[1] / column(total[0:1])
    rcol_ref[...] = rcol * SCALE if second else rcol
    sums_body(second, False, True, seg_ref, w_ref, cols_ref, r1_ref, rcol_ref, edge_ref, parts_ref)


def keep_kernel(second, seg_ref, w_ref, cols_ref, r1_ref, *refs):
    if second:
        r2_ref, edge_ref, sums_ref, give_ref, parts_ref = refs
    else:
        edge_ref, sums_ref, give_ref, parts_ref = refs
        r2_ref = None
    for mine, ends, out_ref in ((True, True, edge_ref), (True, False, sums_ref), (False, False, give_ref)):
        sums_body(second, mine, ends, seg_ref, w_ref, cols_ref, r1_ref, r2_ref, out_ref, parts_ref)


def join(refs):
    rows = refs[0].shape[1]
    name = rows - 3
    sub = lax.broadcasted_iota(jnp.int32, (rows, LANES), 0)
    out = []
    for e, pick in ((0, jnp.minimum), (1, jnp.maximum)):
        names = [ref[e, name : name + 1, :] for ref in refs]
        edge = functools.reduce(pick, names)
        total = jnp.zeros((rows, LANES), jnp.float32)
        for ref, own in zip(refs, names):
            total = total + jnp.where(own == edge, ref[e], 0.0)
        out.append(jnp.where(sub == name, edge, total))
    return out


def chip_kernel(keep_ref, got_ref, chip_ref):
    head, tail = join([keep_ref, got_ref])
    chip_ref[0] = head
    chip_ref[1] = tail


def plane_kernel(*refs):
    send_ref = refs[-1]
    z = lax.axis_index("bg") // PLANE
    head, tail = join(refs[:-1])
    for j in range(send_ref.shape[0]):

        @pl.when(j > z)
        def _():
            send_ref[j] = tail

        @pl.when(j <= z)
        def _():
            send_ref[j] = head


def edge_kernel(keep_ref, got_ref, far_ref, *refs):
    chips, (own_ref, other_ref) = refs[:-2], refs[-2:]
    planes, rows = far_ref.shape[:2]
    me = lax.axis_index("bg")
    z = me // PLANE
    x = (me // 2) % (PLANE // 2)
    core = me % 2
    name = rows - 3
    sub = lax.broadcasted_iota(jnp.int32, (rows, LANES), 0)

    for mine_ref, near_ref, out_ref, side in ((keep_ref, got_ref, own_ref, core), (got_ref, keep_ref, other_ref, 1 - core)):
        for e in range(2):
            county = mine_ref[e, name : name + 1, :]
            total = mine_ref[e]

            def add(total, ref, county=county):
                return total + jnp.where(ref[name : name + 1, :] == county, ref[...], 0.0)

            total = add(total, near_ref.at[side])
            for m, chip_ref in enumerate(chips, 1):
                total = add(total, chip_ref.at[jnp.where((x ^ m) < x, 1, 0)])
            for j in range(planes):
                hit = jnp.logical_and(far_ref[j, name : name + 1, :] == county, j != z)
                total = total + jnp.where(hit, far_ref[j], 0.0)
            out_ref[e] = total


def each_sum(n, edge_ref, sums_ref, body):
    group = 4

    @pl.when(n > 2)
    def _():
        @pl.loop(0, (n + group - 1) // group)
        def _(g):
            for i in range(group):
                body(g * group + i, sums_ref.at[g * group + i])

    body(0, edge_ref.at[0])
    body(n - 1, edge_ref.at[1])


def rows_kernel(mine, seg_ref, w_ref, cols_ref, r1_ref, sums_ref, edge_ref, share_ref, *refs):
    if mine:
        goal_ref, acc_ref, fac_ref = refs
    else:
        part_ref, share_row_ref, goal_ref, msg_ref, fac_ref, acc_ref = refs
    w_ref = w_ref.at[side_of(mine)]
    half = w_ref.shape[1] // LANES
    side = side_of(mine)
    n = seg_counts(seg_ref)[0]

    def factor(k, sum_ref):
        goal = share_ref[k, side] * sum_ref[half : half + 1, :]
        goal_ref[k] = goal
        fac_ref[k] = goal / sum_ref[...]

    each_sum(n, edge_ref, sums_ref, factor)
    acc_ref[...] = jnp.zeros_like(acc_ref) if mine else part_ref[...]

    def pair(k, rows, mask):
        r1 = jnp.where(mask, r1_ref[rows, :], 0.0)
        sums = [None] * 4
        for t in range(half):
            x = w_ref[rows, tile(t)] * r1 * fac_ref[k, t : t + 1, :]
            sums[t % 4] = x if sums[t % 4] is None else sums[t % 4] + x
        acc_ref[rows, :] += (sums[0] + sums[1]) + (sums[2] + sums[3])

    each_pair(seg_ref, cols_ref, pair)
    if not mine:
        message(msg_ref, jnp.sum(acc_ref[...].T, axis=0, keepdims=True), share_row_ref[1:2, :])


def fitted(mine, chunks, done, seg_ref, w_ref, cols_ref, r1_ref, r2_ref, goal_ref, total_ref, sums_ref, edge_ref, out_ref, fac_ref):
    w_ref = w_ref.at[side_of(mine)]
    half = w_ref.shape[1] // LANES
    n = seg_counts(seg_ref)[0]

    lane = lax.broadcasted_iota(jnp.int32, (1, LANES), 1)

    def factor(k, sum_ref):
        whole = jnp.sum(jnp.where(lane == seg_name(seg_ref, k), total_ref[1:2, :], 0.0), axis=1, keepdims=True)
        fac_ref[k] = 100.0 * (goal_ref[k] * ((1.0 / SHARE) / whole) / sum_ref[...])

    each_sum(n, edge_ref, sums_ref, factor)
    for q in range(chunks):
        own = range(q * half // chunks, (q + 1) * half // chunks)

        def pair(k, rows, mask):
            r1 = r1_ref[rows, :]
            r2 = r2_ref[rows, :]
            for t in own:
                x = w_ref[rows, tile(t)] * r1 * r2 * fac_ref[k, t : t + 1, :]
                pltpu.store(out_ref.at[rows, tile(t)], x, mask=mask)

        each_pair(seg_ref, cols_ref, pair)
        done(q)


def last_own_kernel(seg_ref, w_ref, cols_ref, r1_ref, r2_ref, goal_ref, total_ref, sums_ref, edge_ref, out_ref, fac_ref):
    fitted(True, 1, lambda q: None, seg_ref, w_ref, cols_ref, r1_ref, r2_ref, goal_ref, total_ref, sums_ref, edge_ref, out_ref, fac_ref)


def last_kernel(
    chunks, seg_ref, w_ref, cols_ref, r1_ref, r2_ref, goal_ref, total_ref, sums_ref, edge_ref, own_ref, out_hbm, out_ref, fac_ref, sems
):
    width = w_ref.shape[2]
    block = width // chunks

    def place(mine, at, size):
        start = side_of(mine) * width + at
        return out_hbm.at[:, pl.ds(pl.multiple_of(start, LANES), size)]

    copies = []
    for q in range(chunks):
        part = pl.ds(q * block, block)
        copies.append(pltpu.make_async_copy(own_ref.at[:, part], place(True, q * block, block), sems.at[chunks + q]))
        copies[q].start()

    def done(q):
        copy = pltpu.make_async_copy(out_ref.at[:, pl.ds(q * block, block)], place(False, q * block, block), sems.at[q])
        copy.start()
        copies.append(copy)

    fitted(False, chunks, done, seg_ref, w_ref, cols_ref, r1_ref, r2_ref, goal_ref, total_ref, sums_ref, edge_ref, out_ref, fac_ref)
    for copy in copies:
        copy.wait()


def call(kernel, name, ins, in_specs, out_shape, out_specs=None, scratch=()):
    if out_specs is None:
        out_specs = jax.tree.map(lambda _: VMEM, out_shape)
    return pl.pallas_call(
        kernel,
        out_shape=out_shape,
        in_specs=in_specs,
        out_specs=out_specs,
        scratch_shapes=scratch,
        compiler_params=PARAMS,
        cost_estimate=pl.CostEstimate(flops=4 << 20, bytes_accessed=4 << 20, transcendentals=0),
        name=name,
    )(*ins)


def local(planes, parts, seed_slab, row_target, county_id, county_target):
    rows, width = seed_slab.shape
    counties = county_target.shape[0]
    half = width // LANES // 2
    half_rows = half + 4
    out_chunks = 1
    device = planes * PLANE

    edge = f32(2, half_rows, LANES)
    table = f32(counties, half_rows, LANES)
    column_of = f32(rows, LANES)
    small = f32(SUB, LANES)
    parts_scratch = [pltpu.VMEM((half_rows * SUB, LANES), jnp.float32)]
    inputs = (county_id, county_id.reshape(1, rows), row_target.reshape(1, rows), county_target, seed_slab)
    hbm = [pltpu.with_memory_space_constraint(x, pltpu.HBM) for x in inputs]
    msg, slab = call(
        first_kernel,
        "row_sums_1",
        hbm[4:],
        [HBM],
        (small, f32(2, rows, width // 2)),
        None,
        [pltpu.VMEM((rows, LANES), jnp.float32), pltpu.SemaphoreType.DMA((5,))],
    )

    def swap(x, axis, size, mask):
        return lax.ppermute(x, axis, [(i, i ^ mask) for i in range(size)])

    def over_type(x):
        return [x] + [swap(x, "type", parts, m) for m in range(1, parts)]

    lines = [[PLANE * z + s for z in range(planes)] for s in range(PLANE)]

    def edges(give, keep):
        got = swap(give, "bg", device, 1)
        keep = keep()
        chip = call(chip_kernel, "chip_sums", (keep[0], got), [VMEM] * 2, edge)
        chips = [swap(chip, "bg", device, 2 * m) for m in range(1, PLANE // 2)]
        send = call(plane_kernel, "plane_sums", [chip] + chips, [VMEM] * (PLANE // 2), f32(planes, half_rows, LANES))
        far = lax.all_to_all(send, "bg", 0, 0, axis_index_groups=lines)
        own, other = call(edge_kernel, "edge_sums", [keep[0], got, far] + chips, [VMEM] * (2 + PLANE // 2), (edge, edge))
        return own, swap(other, "bg", device, 1), keep[1:]

    msgs = over_type(msg)
    seg, cols, share, share_row = call(
        prepare_kernel,
        "prepare",
        hbm[:4],
        [HBM] * 4,
        (jax.ShapeDtypeStruct((table_rows(counties), LANES), jnp.int32), f32(2, rows, LANES), f32(counties, 2, half_rows, LANES), small),
        None,
        [
            pltpu.SMEM((rows,), jnp.int32),
            pltpu.VMEM((1, rows), jnp.int32),
            pltpu.VMEM((1, rows), jnp.int32),
            pltpu.VMEM((counties, width), jnp.int32),
            pltpu.VMEM((LANES, LANES), jnp.float32),
            pltpu.SemaphoreType.DMA((3 + counties // SUB,)),
        ],
    )
    give, r1 = call(
        functools.partial(give_kernel, False, parts),
        "county_sums_1a",
        [seg] + msgs + [share, slab, cols],
        [VMEM] * (parts + 4),
        (edge, column_of),
        None,
        parts_scratch,
    )
    own, other, (sums_keep, sums_give) = edges(
        give,
        lambda: call(functools.partial(keep_kernel, False), "county_sums_1b", (seg, slab, cols, r1), [VMEM] * 4, (edge, table, table), None, parts_scratch),
    )
    fac = pltpu.VMEM((counties, half_rows, LANES), jnp.float32)
    goal_keep, part = call(
        functools.partial(rows_kernel, True),
        "row_sums_2a",
        (seg, slab, cols, r1, sums_keep, own, share),
        [VMEM] * 7,
        (table, column_of),
        None,
        [fac],
    )
    goal_give, msg = call(
        functools.partial(rows_kernel, False),
        "row_sums_2b",
        (seg, slab, cols, r1, sums_give, other, share, part, share_row),
        [VMEM] * 9,
        (table, small),
        None,
        [fac, pltpu.VMEM((rows, LANES), jnp.float32)],
    )
    give, r2, total = call(
        functools.partial(give_kernel, True, parts),
        "county_sums_2a",
        [seg] + over_type(msg) + [slab, cols, r1],
        [VMEM] * (parts + 4),
        (edge, column_of, small),
        None,
        parts_scratch,
    )
    own, other, (sums_keep, sums_give) = edges(
        give,
        lambda: call(functools.partial(keep_kernel, True), "county_sums_2b", (seg, slab, cols, r1, r2), [VMEM] * 5, (edge, table, table), None, parts_scratch),
    )
    mine = call(
        last_own_kernel,
        "fitted_a",
        (seg, slab, cols, r1, r2, goal_keep, total, sums_keep, own),
        [VMEM] * 9,
        f32(rows, width // 2),
        None,
        [fac],
    )
    return call(
        functools.partial(last_kernel, out_chunks),
        "fitted_b",
        (seg, slab, cols, r1, r2, goal_give, total, sums_give, other, mine),
        [VMEM] * 10,
        f32(rows, width),
        HBM,
        [pltpu.VMEM((rows, width // 2), jnp.float32), fac, pltpu.SemaphoreType.DMA((2 * out_chunks,))],
    )


def solution(mesh):
    return jax.shard_map(
        functools.partial(local, mesh.shape["bg"] // PLANE, mesh.shape["type"]),
        mesh=mesh,
        in_specs=(P("bg", "type"), P("bg"), P("bg"), P(None, "type")),
        out_specs=P("bg", "type"),
        check_vma=False,
    )
```
